256 devices in a mesh: pair: 64 (over y, z_hi, x, core), tok: 4 (over z_lo).
Axes of the slice: x: 4, y: 4, z: 8 (z_hi: 2, z_lo: 4; z = z_hi * 4 + z_lo), core: 2. Of those that a mesh axis runs over, the one named last changes fastest.
Arguments:
- act_vals: bfloat16 [11, 128, 128], P(None, 'tok'), may hold values from 0.5 to 3
- act_idx: int32 [11, 128, 128], replicated, may hold values from 0 to 2047, all different within a row
- slot_pairs: int32 [128, 2], replicated, may hold values from -1 to 10, as said below
- decoders: bfloat16 [128, 2048, 4096], P('pair', None, 'tok'), may hold values from -0.5 to 0.5
- targets: bfloat16 [11, 128, 4096], P(None, 'pair', 'tok'), may hold values from -6 to 6
Outputs:
- feat_grad: float32 [11, 128, 128], P(None, 'pair')
The draws below stay inside these ranges and needn't reach their ends.
Inputs may be any that keep to these rules, and one draw needn't show every extreme that they name: `slot_pairs`: row 2 * i + j is slot j of index i of pair. A live slot holds a source layer and a target layer with source <= target; exactly 64 slots are live and their pairs are distinct; an empty slot holds -1 in both columns. Some index of pair has all of its 2 slots live. `act_idx`: the 128 feature numbers of one layer and token are distinct.
All inputs are finite; a program needn't handle non-finite values.
Results may differ from the reference program's by a relative error of at most 0.00056.
Values may be sent and summed in bfloat16 or wider, within the bound.
A program may use at most 64 MiB of HBM per device.

```python
import jax
import jax.numpy as jnp
from jax import lax

D = 4096
F = 2048
K = 128
L = 11
SLOTS = 2
TOKENS = 128
SLOTS_ALL = 128
N_PAIR = 64


def draw_slot_pairs(key, part):
    slots_all = N_PAIR * SLOTS
    key_pairs = jax.random.fold_in(key, 11)
    key_owner = jax.random.fold_in(key, 23)
    key_slots = jax.random.fold_in(key, 37)
    layer_ids = jnp.arange(L, dtype=jnp.int32)
    source_grid = jnp.broadcast_to(layer_ids[:, None], (L, L)).reshape(-1)
    target_grid = jnp.broadcast_to(layer_ids[None, :], (L, L)).reshape(-1)
    ranking = jax.random.permutation(key_pairs, L * L).astype(jnp.int32)
    scores = jnp.where(source_grid <= target_grid, ranking, ranking + L * L)
    chosen = jnp.argsort(scores, stable=True)[:N_PAIR]
    pair_source = source_grid[chosen]
    pair_target = target_grid[chosen]
    full_owner = jax.random.randint(key_owner, (), 0, N_PAIR, dtype=jnp.int32)
    slot_rank = jax.random.permutation(key_slots, slots_all).astype(jnp.int32)
    owner = jnp.arange(slots_all, dtype=jnp.int32) // SLOTS
    slot_score = slot_rank - jnp.where(owner == full_owner, slots_all, 0)
    ordering = jnp.argsort(slot_score, stable=True)
    position = jnp.argsort(ordering, stable=True).astype(jnp.int32)
    live = position < N_PAIR
    clipped = jnp.minimum(position, N_PAIR - 1)
    source_col = jnp.where(live, pair_source[clipped], -1)
    target_col = jnp.where(live, pair_target[clipped], -1)
    return jnp.stack([source_col, target_col], axis=1).astype(jnp.int32)


def block_scale(key, dims, cuts, low, largest):
    def one(dim, parts):
        draws = jax.random.uniform(jax.random.fold_in(jax.random.fold_in(key, 6), dim), (parts,), jnp.float32, low / len(cuts), largest / len(cuts))
        return jnp.repeat(jnp.exp(draws), dims[dim] // parts).reshape((-1,) + (1,) * (len(dims) - dim - 1))

    loudness = one(*cuts[0])
    for cut in cuts[1:]:
        loudness = loudness * one(*cut)
    return loudness


def choose_distinct(rng, rows, count, top, lift):
    sequence = jax.random.permutation(jax.random.fold_in(rng, 1), count)
    boost = sequence
    for power in range(3):
        boost = boost * boost // count
    boost = boost * lift // count
    tickets = jax.random.randint(jax.random.fold_in(rng, 2), (rows, count), 0, 4096) + boost
    fixed_rows = jax.random.permutation(jax.random.fold_in(rng, 3), rows)[jnp.arange(count) % rows]
    tickets = jnp.where(jnp.arange(rows)[:, None] == fixed_rows[None, :], 1 << 14, tickets)
    priority = tickets * count + jnp.arange(count)
    return lax.top_k(priority.astype(jnp.int32), top)[1].astype(jnp.int32)


def bell_draw(own_key, dims, spread, most, cuts=(), kind=jnp.bfloat16):
    values = spread * jax.random.normal(own_key, dims, jnp.float32)
    if cuts:
        values = values * block_scale(own_key, dims, cuts, -0.22, 0.18)
    return jnp.clip(values, -most, most).astype(kind)


def setup_inputs(seed: int = 0) -> dict:
    streams_of = jax.random.split(jax.random.key(seed), 6)
    return {
        "act_vals": jnp.clip(0.5 + 2.5 * jax.random.uniform(streams_of[0], (L, TOKENS, K), jnp.float32) ** block_scale(streams_of[0], (L, TOKENS, K), ((1, 4),), -0.2, 0.2), 0.5, 3.0).astype(jnp.bfloat16),
        "act_idx": choose_distinct(streams_of[1], L * TOKENS, F, K, 0).reshape((L, TOKENS, K)),
        "slot_pairs": draw_slot_pairs(jax.random.fold_in(streams_of[5], 71), 0),
        "decoders": bell_draw(streams_of[3], (SLOTS_ALL, F, D), K ** -0.5, 0.5, ((0, 64), (2, 4))),
        "targets": bell_draw(streams_of[4], (L, TOKENS, D), 1.0, 6.0, ((1, 64), (2, 4))),
    }


def densify(values, positions, feature_count):
    row_ids = jnp.arange(values.shape[0])[:, None]
    empty_rows = jnp.zeros((values.shape[0], feature_count), jnp.bfloat16)
    return empty_rows.at[row_ids, positions].set(values)


def reference(act_vals, act_idx, slot_pairs, decoders, targets):
    feature_count = decoders.shape[1]
    source_layer = jnp.maximum(slot_pairs[:, 0], 0).astype(jnp.int32)
    target_layer = jnp.maximum(slot_pairs[:, 1], 0).astype(jnp.int32)
    live_flag = (slot_pairs[:, 1] >= 0).astype(jnp.float32)

    def forward(running, record):
        source, target, flag, decoder = record
        dense_rows = densify(act_vals[source], act_idx[source], feature_count)
        partial_value = jnp.dot(dense_rows, decoder, preferred_element_type=jnp.float32)
        return running.at[target].add(flag * partial_value), None

    start_sum = jnp.zeros((L, TOKENS, D), jnp.float32)
    rebuilt, _ = lax.scan(forward, start_sum, (source_layer, target_layer, live_flag, decoders))
    residual = ((rebuilt - targets.astype(jnp.float32)) * D ** -0.5).astype(jnp.bfloat16)

    def backward(running, record):
        source, target, flag, decoder = record
        gradient = lax.dot_general(residual[target], decoder, (((1,), (1,)), ((), ())), preferred_element_type=jnp.float32)
        picked = jnp.take_along_axis(gradient, act_idx[source], axis=1)
        return running.at[source].add(flag * picked), None

    start_grad = jnp.zeros((L, TOKENS, K), jnp.float32)
    result, _ = lax.scan(backward, start_grad, (source_layer, target_layer, live_flag, decoders))
    return result
```

```python
import functools

import jax
import jax.numpy as jnp
from jax import lax
from jax.experimental import pallas as pl
from jax.experimental.pallas import tpu as pltpu
from jax.sharding import PartitionSpec as P

MESH = pl.DeviceIdType.MESH
F32, BF16 = jnp.float32, jnp.bfloat16
L, K, F, D = 11, 128, 2048, 4096
DC = 1024
ROWS = 128
CB = 256
RB = 16


def pair_of(y, zh, x, c):
    return ((y * 2 + zh) * 4 + x) * 2 + c


def kernel(sp, vals, idx, dec_hbm, tg, out, dec, v0, i0, vp, lo, hi, onehot, dense, part, arrived, tgr,
           sums, sums_z, resid, back, grad_in, picked, gsend, grecv, fin, fin_r,
           dec_sem, send_sem, recv_sem):
    pair, tok = lax.axis_index("pair"), lax.axis_index("tok")
    y, zh, x, c = pair // 16, (pair // 8) % 2, (pair // 2) % 4, pair % 2

    def peer(k):
        return (y + k // 8) % 4, (x + (k // 2) % 4) % 4, (c + k) % 2

    def giver(k):
        return (y + 4 - k // 8) % 4, (x + 4 - (k // 2) % 4) % 4, (c + k) % 2

    def remote(src, dst, n, device):
        return pltpu.make_async_remote_copy(src_ref=src, dst_ref=dst, send_sem=send_sem.at[n],
                                            recv_sem=recv_sem.at[n], device_id=device, device_id_type=MESH)

    def dec_copy(j):
        return pltpu.make_async_copy(dec_hbm.at[j], dec.at[j], dec_sem.at[j])

    dec_copy(0).start()
    dec_copy(1).start()

    barrier = pltpu.get_barrier_semaphore()

    def greet(k, _):
        py, px, pc = peer(k)
        pl.semaphore_signal(barrier, inc=1, device_id=(pair_of(py, zh, px, pc), tok), device_id_type=MESH)
        return 0

    lax.fori_loop(1, 32, greet, 0)

    def greet_column(m, _):
        pz, pt = (zh + m // 4) % 2, (tok + m) % 4
        pl.semaphore_signal(barrier, inc=1, device_id=(pair_of(y, pz, x, c), pt), device_id_type=MESH)
        return 0

    lax.fori_loop(1, 8, greet_column, 0)

    for j in range(2):
        layer = jnp.maximum(sp[0, 2 * pair + j], 0)
        v0[j, pl.ds(pl.multiple_of(tok * 32, 32), 32), :] = vals[layer]
        i0[j] = idx[layer]
    pl.semaphore_wait(barrier, 38)

    mine = pl.ds(pl.multiple_of(tok * 32, 32), 32)
    for d in range(1, 4):
        remote(v0.at[:, mine], v0.at[:, mine], 0, (pair, (tok + d) % 4)).start()

    def send_targets(px, _):
        cols = pl.ds(px * 2, 2)
        here = jnp.logical_and(px == x, c == zh)

        @pl.when(jnp.logical_not(here))
        def _():
            remote(tg.at[cols], tgr.at[x * 2 + c], 1, (pair_of(y, zh, px, zh), tok)).start()

        @pl.when(here)
        def _():
            tgr[x * 2 + c] = tg[cols]

        return 0

    lax.fori_loop(0, 4, send_targets, 0)

    pltpu.make_async_remote_copy(src_ref=v0.at[:, pl.ds(0, 96)], dst_ref=v0.at[:, pl.ds(0, 96)],
                                 send_sem=send_sem.at[0], recv_sem=recv_sem.at[0],
                                 device_id=(pair, (tok + 1) % 4), device_id_type=MESH).wait_recv()

    for j in range(2):
        vp[...] = v0[j].astype(F32)
        for gb in range(16):
            g, b = gb // 2, gb % 2
            rows = i0[j, pl.ds(g * 16 + b, 8, stride=2), :]
            lo[j, gb * 8:gb * 8 + 8, :] = jnp.bitwise_and(rows, 127)
            hi[j, gb * 8:gb * 8 + 8, :] = lax.shift_right_logical(rows, 7)

        def two_rows(i, _):
            lefts, rights = [], []
            for u in range(2):
                r = i * 2 + u
                n = (r // 16) * 16 + (r % 8) * 2 + (r // 8) % 2
                low = jnp.broadcast_to(lo[j, pl.ds(r, 1), :], (128, K))
                high = jnp.broadcast_to(hi[j, pl.ds(r, 1), :], (16, K))
                value = jnp.broadcast_to(vp[pl.ds(n, 1), :], (16, K))
                rights.append(jnp.where(low == lax.broadcasted_iota(jnp.int32, (128, K), 0), 1.0, 0.0).astype(BF16))
                lefts.append(jnp.where(high == lax.broadcasted_iota(jnp.int32, (16, K), 0), value, 0.0).astype(BF16))
            nothing = jnp.zeros((16, K), BF16)
            left = jnp.concatenate([jnp.concatenate([lefts[0], nothing], 1),
                                    jnp.concatenate([nothing, lefts[1]], 1)], 0)
            right = jnp.concatenate(rights, 1)
            onehot[pl.ds(pl.multiple_of(i * 32, 32), 32), :] = lax.dot_general(
                left, right, (((1,), (1,)), ((), ())), preferred_element_type=F32)
            return 0

        lax.fori_loop(0, 64, two_rows, 0)
        for h in range(16):
            dense[j, :, h * 128:h * 128 + 128] = onehot[pl.ds(h, ROWS, stride=16), :].astype(BF16)

        dec_copy(j).wait()

        def column_block(i, _):
            px = (x + i) % 4
            part[j, px] = jnp.dot(dense[j], dec[j, :, pl.ds(pl.multiple_of(px * CB, CB), CB)],
                                  preferred_element_type=F32)

            def send_block(m, _):
                py, pc = (y + m // 2) % 4, (c + m) % 2
                k = ((m // 2) * 4 + i) * 2 + m % 2
                rows = pl.ds(pl.multiple_of((py * 2 + pc) * RB, RB), RB)

                @pl.when(k != 0)
                def _():
                    remote(part.at[j, px, rows], arrived.at[j, k], 2 + j, (pair_of(py, zh, px, pc), tok)).start()

                @pl.when(k == 0)
                def _():
                    arrived[j, k] = part[j, px, rows, :]

                return 0

            lax.fori_loop(0, 8, send_block, 0)
            return 0

        lax.fori_loop(0, 4, column_block, 0)

    for l in range(L):
        sums[l] = jnp.zeros((RB, CB), F32)

    @pl.when(c == zh)
    def _():
        wait_blocks = pltpu.make_async_remote_copy(
            src_ref=tgr.at[pl.ds(0, 7)], dst_ref=tgr.at[pl.ds(0, 7)], send_sem=send_sem.at[1],
            recv_sem=recv_sem.at[1], device_id=(pair, (tok + 1) % 4), device_id_type=MESH)
        wait_blocks.wait_recv()

        def minus(l, _):
            for b in range(2):
                for q in range(2):
                    sums[l, b * 8:b * 8 + 8, q * 128:q * 128 + 128] = -tgr.reshape(8 * 48, 128)[
                        pl.ds(q * 24 + l * 2 + b, 8, stride=48), :]
            return 0

        lax.fori_loop(0, L, minus, 0)

    for j in range(2):
        blocks = arrived.at[j, pl.ds(1, 31)]
        pltpu.make_async_remote_copy(src_ref=blocks, dst_ref=blocks, send_sem=send_sem.at[2 + j],
                                     recv_sem=recv_sem.at[2 + j], device_id=(pair, (tok + 1) % 4),
                                     device_id_type=MESH).wait_recv()
        for half in range(2):
            def add(k, totals):
                gy, gx, gc = giver(k)
                target = sp[1, 2 * pair_of(gy, zh, gx, gc) + j]
                block = arrived[j, k, half * 8:half * 8 + 8, :]
                return tuple(t + jnp.where(target == l, block, 0.0) for l, t in enumerate(totals))

            totals = lax.fori_loop(0, 32, add, tuple(sums[l, half * 8:half * 8 + 8, :] for l in range(L)))
            for l in range(L):
                sums[l, half * 8:half * 8 + 8, :] = totals[l]

    exchange = remote(sums, sums_z, 4, (pair_of(y, 1 - zh, x, c), tok))
    exchange.start()
    exchange.wait()
    for l in range(L):
        resid[l] = ((sums[l] + sums_z[l]) * D ** (-0.5)).astype(BF16)

    my_rows = pl.ds(pl.multiple_of((y * 2 + c) * RB, RB), RB)
    my_cols = pl.ds(pl.multiple_of(x * CB, CB), CB)
    for j in range(2):
        def give_back(k, _):
            py, px, pc = peer(k)
            to = pair_of(py, zh, px, pc)
            back[j, k] = resid[jnp.maximum(sp[1, 2 * to + j], 0)]

            @pl.when(k != 0)
            def _():
                remote(back.at[j, k], grad_in.at[j, my_rows, my_cols], 5 + j, (to, tok)).start()

            return 0

        lax.fori_loop(0, 32, give_back, 0)
        grad_in[j, my_rows, my_cols] = back[j, 0]

    for j in range(2):
        blocks = back.at[j, pl.ds(1, 31)]
        pltpu.make_async_remote_copy(src_ref=blocks, dst_ref=blocks, send_sem=send_sem.at[5 + j],
                                     recv_sem=recv_sem.at[5 + j], device_id=(pair, (tok + 1) % 4),
                                     device_id_type=MESH).wait_recv()
        picked[...] = jnp.zeros((ROWS, K), F32)

        def features(f, _):
            grads = lax.dot_general(grad_in[j], dec[j, pl.ds(pl.multiple_of(f * 256, 256), 256), :],
                                    (((1,), (1,)), ((), ())), preferred_element_type=F32)
            for q in range(2):
                chosen = jnp.take_along_axis(grads[:, q * 128:q * 128 + 128], lo[j], axis=1)
                picked[...] = jnp.where(hi[j] == f * 2 + q, chosen, picked[...])
            return 0

        lax.fori_loop(0, 8, features, 0)
        for gb in range(16):
            start = (gb // 4) * 64 + j * 4 + gb % 4
            gsend.reshape(256, K)[pl.ds(start, 8, stride=8), :] = picked[gb * 8:gb * 8 + 8, :]

    def send_picked(k, _):
        py, px, pc = peer(k)
        q = (py * 4 + px) * 2 + pc

        @pl.when(k != 0)
        def _():
            remote(gsend.at[q], grecv.at[k], 7, (pair_of(py, zh, px, pc), tok)).start()

        @pl.when(k == 0)
        def _():
            grecv[k] = gsend[q]

        return 0

    lax.fori_loop(0, 32, send_picked, 0)
    blocks = grecv.at[pl.ds(1, 31)]
    pltpu.make_async_remote_copy(src_ref=blocks, dst_ref=blocks, send_sem=send_sem.at[7], recv_sem=recv_sem.at[7],
                                 device_id=(pair, (tok + 1) % 4), device_id_type=MESH).wait_recv()

    def add_picked(k, totals):
        gy, gx, gc = giver(k)
        first = 2 * pair_of(gy, zh, gx, gc)
        upper = lax.broadcasted_iota(jnp.int32, (8, K), 0) < 4
        source = jnp.where(upper, sp[0, first], sp[0, first + 1])
        block = grecv[k]
        return tuple(t + jnp.where(source == l, block, 0.0) for l, t in enumerate(totals))

    totals = lax.fori_loop(0, 32, add_picked, tuple(jnp.zeros((8, K), F32) for _ in range(L)))
    for l in range(L):
        both = totals[l][0:4] + totals[l][4:8]
        fin[0, 2 * l:2 * l + 2, :] = both[0:2]
        fin[1, 2 * l:2 * l + 2, :] = both[2:4]
    for z in range(2):
        fin[z, 22:24, :] = jnp.zeros((2, K), F32)

    me = zh * 4 + tok

    def send_final(m, _):
        pz, pt = (zh + m // 4) % 2, (tok + m) % 4
        remote(fin.at[pz], fin_r.at[me], 8, (pair_of(y, pz, x, c), pt)).start()
        return 0

    lax.fori_loop(1, 8, send_final, 0)
    fin_r[me] = fin[zh]
    blocks = fin_r.at[pl.ds(0, 7)]
    pltpu.make_async_remote_copy(src_ref=blocks, dst_ref=blocks, send_sem=send_sem.at[8], recv_sem=recv_sem.at[8],
                                 device_id=(pair, (tok + 1) % 4), device_id_type=MESH).wait_recv()
    total = fin_r[0]
    for m in range(1, 8):
        total = total + fin_r[m]
    out[...] = total

    def sent(ref, n):
        pltpu.make_async_remote_copy(src_ref=ref, dst_ref=ref, send_sem=send_sem.at[n], recv_sem=recv_sem.at[n],
                                     device_id=(pair, (tok + 1) % 4), device_id_type=MESH).wait_send()

    sent(v0.at[:, pl.ds(0, 96)], 0)

    @pl.when(c == zh)
    def _():
        sent(tgr.at[pl.ds(0, 3)], 1)

    @pl.when(c != zh)
    def _():
        sent(tgr.at[pl.ds(0, 4)], 1)

    for j in range(2):
        sent(arrived.at[j, pl.ds(1, 31)], 2 + j)
        sent(back.at[j, pl.ds(1, 31)], 5 + j)
    sent(grecv.at[pl.ds(1, 31)], 7)
    sent(fin_r.at[pl.ds(0, 7)], 8)


def local(act_vals, act_idx, slot_pairs, decoders, targets):
    tg = jnp.pad(targets.astype(F32).reshape(2 * L, 8, 128), ((0, 2), (0, 0), (0, 0))).transpose(1, 0, 2)
    vmem = pl.BlockSpec(memory_space=pltpu.VMEM)
    out = pl.pallas_call(
        kernel,
        out_shape=jax.ShapeDtypeStruct((24, K), F32),
        in_specs=[pl.BlockSpec(memory_space=pltpu.SMEM), vmem, vmem, pl.BlockSpec(memory_space=pl.ANY), vmem],
        out_specs=vmem,
        scratch_shapes=[
            pltpu.VMEM((2, F, DC), BF16),
            pltpu.VMEM((2, ROWS, K), BF16),
            pltpu.VMEM((2, ROWS, K), jnp.int32),
            pltpu.VMEM((ROWS, K), F32),
            pltpu.VMEM((2, ROWS, K), jnp.int32),
            pltpu.VMEM((2, ROWS, K), jnp.int32),
            pltpu.VMEM((ROWS * 16, K), F32),
            pltpu.VMEM((2, ROWS, F), BF16),
            pltpu.VMEM((2, 4, ROWS, CB), F32),
            pltpu.VMEM((2, 32, RB, CB), F32),
            pltpu.VMEM((8, 2, 24, 128), F32),
            pltpu.VMEM((L, RB, CB), F32),
            pltpu.VMEM((L, RB, CB), F32),
            pltpu.VMEM((L, RB, CB), BF16),
            pltpu.VMEM((2, 32, RB, CB), BF16),
            pltpu.VMEM((2, ROWS, DC), BF16),
            pltpu.VMEM((ROWS, K), F32),
            pltpu.VMEM((32, 8, K), F32),
            pltpu.VMEM((32, 8, K), F32),
            pltpu.VMEM((2, 24, K), F32),
            pltpu.VMEM((8, 24, K), F32),
            pltpu.SemaphoreType.DMA((2,)),
            pltpu.SemaphoreType.DMA((9,)),
            pltpu.SemaphoreType.DMA((9,)),
        ],
        compiler_params=pltpu.CompilerParams(collective_id=0, has_side_effects=True, vmem_limit_bytes=48 << 20),
        cost_estimate=pl.CostEstimate(flops=2 * 2 * 2 * ROWS * F * DC, bytes_accessed=10 << 20, transcendentals=0),
        name="transcoder",
    )(slot_pairs.T, act_vals, act_idx, decoders, tg)
    return out[:2 * L].reshape(L, 2, K)


def solution(mesh):
    return jax.shard_map(
        local,
        mesh=mesh,
        in_specs=(P(None, "tok", None), P(), P(), P("pair", None, "tok"), P(None, "pair", "tok")),
        out_specs=P(None, "pair", None),
        check_vma=False,
    )
```

```python
import functools

import jax
import jax.numpy as jnp
from jax import lax
from jax.experimental import pallas as pl
from jax.experimental.pallas import tpu as pltpu
from jax.sharding import PartitionSpec as P

MESH = pl.DeviceIdType.MESH
F32, BF16, I32 = jnp.float32, jnp.bfloat16, jnp.int32
NT = (((1,), (1,)), ((), ()))
L, K, F, D = 11, 128, 2048, 4096
DC = 1024
ROWS = 128
CB = 256
RB = 16
UNROLL = 16


def place_maps(j, lo, hi, onehot, inv):
    nothing = jnp.zeros((16, K), BF16)
    lows = lax.broadcasted_iota(I32, (128, K), 0).astype(F32).astype(BF16)
    highs = lax.broadcasted_iota(I32, (16, K), 0)
    places = lax.broadcasted_iota(I32, (16, K), 1) + 1

    def masks(r):
        low = jnp.broadcast_to(lo[j, pl.ds(r, 1), :].astype(F32).astype(BF16), (128, K))
        high = jnp.broadcast_to(hi[j, pl.ds(r, 1), :], (16, K))
        return (jnp.where(high == highs, places, 0).astype(F32).astype(BF16),
                jnp.where(low == lows, jnp.ones((), BF16), jnp.zeros((), BF16)))

    def rows(i, _):
        for u in range(UNROLL):
            r = i * (2 * UNROLL) + 2 * u
            (left0, right0), (left1, right1) = masks(r), masks(r + 1)
            left = jnp.concatenate([jnp.concatenate([left0, nothing], 1), jnp.concatenate([nothing, left1], 1)], 0)
            onehot[pl.ds(pl.multiple_of(r * 16, 32), 32), :] = lax.dot_general(
                left, jnp.concatenate([right0, right1], 1), NT, preferred_element_type=F32)
        return 0

    lax.fori_loop(0, 64 // UNROLL, rows, 0)
    for h in range(16):
        inv[j, h] = onehot[pl.ds(h, ROWS, stride=16), :].astype(I32)


def kernel(sp_hbm, vals_hbm, idx_hbm, dec_hbm, tg_hbm, out, sp, vals, idx, tg_ref, dec, v0, i0, vp, lo, hi, onehot, inv,
           dense, part, arrived, tg, tgr, sums, sums_z, resid, back, grad_in, picked, gsend, grecv, fin, fin_r,
           loc_sem, send_sem, recv_sem):
    pair, tok = lax.axis_index("pair"), lax.axis_index("tok")
    y, zh, x, c = pair >> 4, (pair >> 3) & 1, (pair >> 1) & 3, pair & 1

    def mate(k):
        return pair ^ (((k & 24) << 1) | (k & 7))

    def remote(src, dst, n, device):
        return pltpu.make_async_remote_copy(src_ref=src, dst_ref=dst, send_sem=send_sem.at[n],
                                            recv_sem=recv_sem.at[n], device_id=device, device_id_type=MESH)

    def whole(ref, n):
        return remote(ref, ref, n, (pair ^ 1, tok))

    leaving = []

    def finish():
        for ref, n in leaving:
            whole(ref, n).wait_send()

    sp_copy = pltpu.make_async_copy(sp_hbm, sp, loc_sem.at[2])
    vals_copy = pltpu.make_async_copy(vals_hbm, vals, loc_sem.at[3])
    idx_copy = pltpu.make_async_copy(idx_hbm, idx, loc_sem.at[4])
    tg_copy = pltpu.make_async_copy(tg_hbm, tg_ref, loc_sem.at[5])
    dec_copy = [pltpu.make_async_copy(dec_hbm.at[j], dec.at[j], loc_sem.at[j]) for j in range(2)]
    sp_copy.start()
    vals_copy.start()
    idx_copy.start()
    tg_copy.start()
    dec_copy[0].start()
    dec_copy[1].start()

    barrier = pltpu.get_barrier_semaphore()

    def greet_column(m, _):
        pl.semaphore_signal(barrier, inc=1, device_id=(pair ^ ((m & 4) << 1), tok ^ (m & 3)), device_id_type=MESH)
        return 0

    lax.fori_loop(1, 8, greet_column, 0)

    def greet(k, _):
        pl.semaphore_signal(barrier, inc=1, device_id=(mate(k), tok), device_id_type=MESH)
        return 0

    lax.fori_loop(1, 32, greet, 0)

    sp_copy.wait()
    idx_copy.wait()
    for j in range(2):
        i0[...] = idx[jnp.maximum(sp[0, 2 * pair + j], 0)]
        for gb in range(16):
            rows = i0[pl.ds((gb // 2) * 16 + gb % 2, 8, stride=2), :]
            lo[j, gb * 8:gb * 8 + 8, :] = jnp.bitwise_and(rows, 127)
            hi[j, gb * 8:gb * 8 + 8, :] = lax.shift_right_logical(rows, 7)
    place_maps(0, lo, hi, onehot, inv)

    tg_copy.wait()
    for b in range(8):
        for l in range(L):
            tg[b, 2 * l:2 * l + 2, :] = tg_ref[l, :, b * 128:b * 128 + 128].astype(F32)
        tg[b, 22:24, :] = jnp.zeros((2, 128), F32)
    mine = pl.ds(pl.multiple_of(tok * 32, 32), 32)
    vals_copy.wait()
    for j in range(2):
        v0[j, mine, :] = vals[jnp.maximum(sp[0, 2 * pair + j], 0)]

    pl.semaphore_wait(barrier, 38)

    for d in range(1, 4):
        remote(v0.at[:, mine], v0.at[:, mine], 0, (pair, tok ^ d)).start()
    leaving.append((v0.at[:, pl.ds(0, 96)], 0))

    def send_targets(i, _):
        px = x ^ i
        cols = pl.ds(px * 2, 2)

        @pl.when(i != 0)
        def _():
            remote(tg.at[cols], tgr.at[x * 2 + c], 1, ((pair & 56) | (px << 1) | zh, tok)).start()

        @pl.when(jnp.logical_and(i == 0, c != zh))
        def _():
            remote(tg.at[cols], tgr.at[x * 2 + c], 1, (pair ^ 1, tok)).start()

        @pl.when(jnp.logical_and(i == 0, c == zh))
        def _():
            tgr[x * 2 + c] = tg[cols]

        return 0

    lax.fori_loop(0, 4, send_targets, 0)
    place_maps(1, lo, hi, onehot, inv)
    whole(v0.at[:, pl.ds(0, 96)], 0).wait_recv()

    for j in range(2):
        vp[...] = v0[j].astype(F32)

        def spread(g, _):
            rows = pl.ds(pl.multiple_of(g * 16, 16), 16)
            values = jnp.concatenate([vp[pl.ds(g * 16 + b, 8, stride=2), :] for b in range(2)], 0)
            for h in range(16):
                place = inv[j, h, rows, :]
                chosen = jnp.take_along_axis(values, jnp.maximum(place - 1, 0), axis=1)
                dense[rows, h * 128:h * 128 + 128] = jnp.where(place > 0, chosen, 0.0).astype(BF16)
            return 0

        lax.fori_loop(0, 8, spread, 0)
        dec_copy[j].wait()

        def column_block(i, _):
            px = x ^ i
            part[j, px] = jnp.dot(dense[...], dec[j, :, pl.ds(pl.multiple_of(px * CB, CB), CB)],
                                  preferred_element_type=F32)

            def send_block(m, _):
                to = pair ^ ((i << 1) | ((m & 6) << 3) | (m & 1))
                rows = pl.ds(pl.multiple_of((((to >> 4) << 1) | (to & 1)) * RB, RB), RB)

                @pl.when((i | m) != 0)
                def _():
                    remote(part.at[j, px, rows], arrived.at[j, i, m], 9 + j * 4 + i, (to, tok)).start()

                @pl.when((i | m) == 0)
                def _():
                    arrived[j, 0, 0] = part[j, px, rows, :]

                return 0

            lax.fori_loop(0, 8, send_block, 0)
            return 0

        lax.fori_loop(0, 4, column_block, 0)
        for i in range(4):
            leaving.append((arrived.at[j, i, pl.ds(0 if i else 1, 8 if i else 7)], 9 + j * 4 + i))

    sums[...] = jnp.zeros((L, RB, CB), F32)

    @pl.when(c == zh)
    def _():
        whole(tgr.at[pl.ds(0, 7)], 1).wait_recv()
        for l in range(L):
            for b in range(2):
                for q in range(2):
                    sums[l, b * 8:b * 8 + 8, q * 128:q * 128 + 128] = -tgr.reshape(8 * 48, 128)[
                        pl.ds(q * 24 + l * 2 + b, 8, stride=48), :]

    for j in range(2):
        for i in range(4):
            whole(arrived.at[j, i, pl.ds(0 if i else 1, 8 if i else 7)], 9 + j * 4 + i).wait_recv()
            for half in range(2):
                def add(m, totals):
                    source = pair ^ ((i << 1) | ((m & 6) << 3) | (m & 1))
                    target = sp[1, 2 * source + j]
                    block = arrived[j, i, m, half * 8:half * 8 + 8, :]
                    return tuple(t + jnp.where(target == l, block, 0.0) for l, t in enumerate(totals))

                totals = lax.fori_loop(0, 8, add, tuple(sums[l, half * 8:half * 8 + 8, :] for l in range(L)),
                                       unroll=2)
                for l in range(L):
                    sums[l, half * 8:half * 8 + 8, :] = totals[l]

    def sent_targets():
        @pl.when(c == zh)
        def _():
            whole(tgr.at[pl.ds(0, 3)], 1).wait_send()

        @pl.when(c != zh)
        def _():
            whole(tgr.at[pl.ds(0, 4)], 1).wait_send()

    exchange = remote(sums, sums_z, 2, (pair ^ 8, tok))
    exchange.start()
    sent_targets()
    exchange.wait()
    for l in range(L):
        resid[l] = ((sums[l] + sums_z[l]) * D ** (-0.5)).astype(BF16)

    my_rows = pl.ds(pl.multiple_of(((y << 1) | c) * RB, RB), RB)
    my_cols = pl.ds(pl.multiple_of(x * CB, CB), CB)
    for j in range(2):
        def give_back(k, _):
            to = mate(k)
            back[j, k] = resid[jnp.maximum(sp[1, 2 * to + j], 0)]
            remote(back.at[j, k], grad_in.at[j, my_rows, my_cols], 3 + j, (to, tok)).start()
            return 0

        lax.fori_loop(1, 32, give_back, 0)
        grad_in[j, my_rows, my_cols] = resid[jnp.maximum(sp[1, 2 * pair + j], 0)]
        leaving.append((back.at[j, pl.ds(1, 31)], 3 + j))

    for j in range(2):
        whole(back.at[j, pl.ds(1, 31)], 3 + j).wait_recv()
        picked[...] = jnp.zeros((ROWS, K), F32)

        def features(f, _):
            grads = lax.dot_general(grad_in[j], dec[j, pl.ds(pl.multiple_of(f * 256, 256), 256), :],
                                    NT, preferred_element_type=F32)
            for q in range(2):
                chosen = jnp.take_along_axis(grads[:, q * 128:q * 128 + 128], lo[j], axis=1)
                picked[...] = jnp.where(hi[j] == f * 2 + q, chosen, picked[...])
            return 0

        lax.fori_loop(0, 8, features, 0)
        for gb in range(16):
            start = (gb // 4) * 64 + j * 4 + gb % 4
            gsend.reshape(256, K)[pl.ds(start, 8, stride=8), :] = picked[gb * 8:gb * 8 + 8, :]

    def send_picked(k, _):
        to = mate(k)
        q = ((to >> 4) << 3) | (to & 7)
        remote(gsend.at[q], grecv.at[k], 5, (to, tok)).start()
        return 0

    lax.fori_loop(1, 32, send_picked, 0)
    grecv[0] = gsend[(y << 3) | (x << 1) | c]
    leaving.append((grecv.at[pl.ds(1, 31)], 5))
    whole(grecv.at[pl.ds(1, 31)], 5).wait_recv()

    def add_picked(k, totals):
        first = 2 * mate(k)
        upper = lax.broadcasted_iota(I32, (8, K), 0) < 4
        source = jnp.where(upper, sp[0, first], sp[0, first + 1])
        block = grecv[k]
        return tuple(t + jnp.where(source == l, block, 0.0) for l, t in enumerate(totals))

    totals = lax.fori_loop(0, 32, add_picked, tuple(jnp.zeros((8, K), F32) for _ in range(L)), unroll=2)
    for l in range(L):
        both = totals[l][0:4] + totals[l][4:8]
        fin[0, 2 * l:2 * l + 2, :] = both[0:2]
        fin[1, 2 * l:2 * l + 2, :] = both[2:4]
    for z in range(2):
        fin[z, 22:24, :] = jnp.zeros((2, K), F32)

    me = (zh << 2) | tok

    def send_final(m, _):
        remote(fin.at[zh ^ (m >> 2)], fin_r.at[me], 6, (pair ^ ((m & 4) << 1), tok ^ (m & 3))).start()
        return 0

    lax.fori_loop(1, 8, send_final, 0)
    fin_r[me] = fin[zh]
    whole(fin_r.at[pl.ds(0, 7)], 6).wait_recv()
    leaving.append((fin_r.at[pl.ds(0, 7)], 6))
    total = fin_r[0]
    for m in range(1, 8):
        total = total + fin_r[m]
    for l in range(L):
        out[l] = total[2 * l:2 * l + 2]
    finish()


def local(act_vals, act_idx, slot_pairs, decoders, targets):
    hbm, vmem = pl.BlockSpec(memory_space=pltpu.HBM), pl.BlockSpec(memory_space=pltpu.VMEM)
    return pl.pallas_call(
        kernel,
        out_shape=jax.ShapeDtypeStruct((L, 2, K), F32),
        in_specs=[hbm] * 5,
        out_specs=vmem,
        scratch_shapes=[
            pltpu.SMEM((2, 128), I32),
            pltpu.VMEM((L, 32, K), BF16),
            pltpu.VMEM((L, ROWS, K), I32),
            pltpu.VMEM((L, 2, DC), BF16),
            pltpu.VMEM((2, F, DC), BF16),
            pltpu.VMEM((2, ROWS, K), BF16),
            pltpu.VMEM((ROWS, K), I32),
            pltpu.VMEM((ROWS, K), F32),
            pltpu.VMEM((2, ROWS, K), I32),
            pltpu.VMEM((2, ROWS, K), I32),
            pltpu.VMEM((ROWS * 16, K), F32),
            pltpu.VMEM((2, 16, ROWS, K), I32),
            pltpu.VMEM((ROWS, F), BF16),
            pltpu.VMEM((2, 4, ROWS, CB), F32),
            pltpu.VMEM((2, 4, 8, RB, CB), F32),
            pltpu.VMEM((8, 24, 128), F32),
            pltpu.VMEM((8, 2, 24, 128), F32),
            pltpu.VMEM((L, RB, CB), F32),
            pltpu.VMEM((L, RB, CB), F32),
            pltpu.VMEM((L, RB, CB), BF16),
            pltpu.VMEM((2, 32, RB, CB), BF16),
            pltpu.VMEM((2, ROWS, DC), BF16),
            pltpu.VMEM((ROWS, K), F32),
            pltpu.VMEM((32, 8, K), F32),
            pltpu.VMEM((32, 8, K), F32),
            pltpu.VMEM((2, 24, K), F32),
            pltpu.VMEM((8, 24, K), F32),
            pltpu.SemaphoreType.DMA((6,)),
            pltpu.SemaphoreType.DMA((17,)),
            pltpu.SemaphoreType.DMA((17,)),
        ],
        compiler_params=pltpu.CompilerParams(collective_id=0, has_side_effects=True, vmem_limit_bytes=60 << 20),
        cost_estimate=pl.CostEstimate(flops=2 * 2 * 2 * ROWS * F * DC, bytes_accessed=10 << 20, transcendentals=0),
        name="transcoder",
    )(slot_pairs.T, act_vals, act_idx, decoders, targets)


def solution(mesh):
    return jax.shard_map(
        local,
        mesh=mesh,
        in_specs=(P(None, "tok", None), P(), P(), P("pair", None, "tok"), P(None, "pair", "tok")),
        out_specs=P(None, "pair", None),
        check_vma=False,
    )
```

```python
import functools

import jax
import jax.numpy as jnp
from jax import lax
from jax.experimental import pallas as pl
from jax.experimental.pallas import tpu as pltpu
from jax.sharding import PartitionSpec as P

MESH = pl.DeviceIdType.MESH
F32, BF16, I32 = jnp.float32, jnp.bfloat16, jnp.int32
NT = (((1,), (1,)), ((), ()))
L, K, F, D = 11, 128, 2048, 4096
DC = 1024
ROWS = 128
CB = 256
HB = 128
RB = 16
UNROLL = 16


def place_maps(j, lo, hi, onehot, inv):
    nothing = jnp.zeros((16, K), BF16)
    lows = lax.broadcasted_iota(I32, (128, K), 0).astype(F32).astype(BF16)
    highs = lax.broadcasted_iota(I32, (16, K), 0)
    places = lax.broadcasted_iota(I32, (16, K), 1) + 1

    def masks(r):
        low = jnp.broadcast_to(lo[j, pl.ds(r, 1), :].astype(F32).astype(BF16), (128, K))
        high = jnp.broadcast_to(hi[j, pl.ds(r, 1), :], (16, K))
        return (jnp.where(high == highs, places, 0).astype(F32).astype(BF16),
                jnp.where(low == lows, jnp.ones((), BF16), jnp.zeros((), BF16)))

    def rows(i, _):
        for u in range(UNROLL):
            r = i * (2 * UNROLL) + 2 * u
            (left0, right0), (left1, right1) = masks(r), masks(r + 1)
            left = jnp.concatenate([jnp.concatenate([left0, nothing], 1), jnp.concatenate([nothing, left1], 1)], 0)
            onehot[pl.ds(pl.multiple_of(r * 16, 32), 32), :] = lax.dot_general(
                left, jnp.concatenate([right0, right1], 1), NT, preferred_element_type=F32)
        return 0

    lax.fori_loop(0, 64 // UNROLL, rows, 0)
    for h in range(16):
        inv[j, h] = onehot[pl.ds(h, ROWS, stride=16), :].astype(I32)


def kernel(sp_hbm, vals_hbm, idx_hbm, dec_hbm, tg_hbm, out, sp, vals, idx, tg_ref, dec, v0, i0, vp, lo, hi, onehot, inv,
           dense, dect, part, arrived, tg, tgr, sums, sums_z, resid, back, grad_in, picked, gsend, grecv, fin, fin_r,
           loc_sem, send_sem, recv_sem):
    pair, tok = lax.axis_index("pair"), lax.axis_index("tok")
    y, zh, x, c = pair >> 4, (pair >> 3) & 1, (pair >> 1) & 3, pair & 1

    def mate(k):
        return pair ^ (((k & 24) << 1) | (k & 7))

    def remote(src, dst, n, device):
        return pltpu.make_async_remote_copy(src_ref=src, dst_ref=dst, send_sem=send_sem.at[n],
                                            recv_sem=recv_sem.at[n], device_id=device, device_id_type=MESH)

    def whole(ref, n):
        return remote(ref, ref, n, (pair ^ 1, tok))

    leaving = []

    def finish():
        for ref, n in leaving:
            whole(ref, n).wait_send()

    sp_copy = pltpu.make_async_copy(sp_hbm, sp, loc_sem.at[2])
    vals_copy = pltpu.make_async_copy(vals_hbm, vals, loc_sem.at[3])
    idx_copy = pltpu.make_async_copy(idx_hbm, idx, loc_sem.at[4])
    tg_copy = pltpu.make_async_copy(tg_hbm, tg_ref, loc_sem.at[5])
    dec_copy = [pltpu.make_async_copy(dec_hbm.at[j], dec.at[j], loc_sem.at[j]) for j in range(2)]
    sp_copy.start()
    vals_copy.start()
    idx_copy.start()
    tg_copy.start()
    dec_copy[0].start()
    dec_copy[1].start()

    barrier = pltpu.get_barrier_semaphore()

    def greet_column(m, _):
        pl.semaphore_signal(barrier, inc=1, device_id=(pair ^ ((m & 4) << 1), tok ^ (m & 3)), device_id_type=MESH)
        return 0

    lax.fori_loop(1, 8, greet_column, 0)

    def greet(k, _):
        pl.semaphore_signal(barrier, inc=1, device_id=(mate(k), tok), device_id_type=MESH)
        return 0

    lax.fori_loop(1, 32, greet, 0)

    sp_copy.wait()
    idx_copy.wait()
    for j in range(2):
        i0[...] = idx[jnp.maximum(sp[0, 2 * pair + j], 0)]
        for gb in range(16):
            rows = i0[pl.ds((gb // 2) * 16 + gb % 2, 8, stride=2), :]
            lo[j, gb * 8:gb * 8 + 8, :] = jnp.bitwise_and(rows, 127)
            hi[j, gb * 8:gb * 8 + 8, :] = lax.shift_right_logical(rows, 7)
    place_maps(0, lo, hi, onehot, inv)

    tg_copy.wait()
    for b in range(8):
        for l in range(L):
            tg[b, 2 * l:2 * l + 2, :] = tg_ref[l, :, b * 128:b * 128 + 128].astype(F32)
        tg[b, 22:24, :] = jnp.zeros((2, 128), F32)
    mine = pl.ds(pl.multiple_of(tok * 32, 32), 32)
    vals_copy.wait()
    for j in range(2):
        v0[j, mine, :] = vals[jnp.maximum(sp[0, 2 * pair + j], 0)]

    pl.semaphore_wait(barrier, 38)

    for d in range(1, 4):
        remote(v0.at[:, mine], v0.at[:, mine], 0, (pair, tok ^ d)).start()
    leaving.append((v0.at[:, pl.ds(0, 96)], 0))

    def send_targets(i, _):
        px = x ^ i
        cols = pl.ds(px * 2, 2)

        @pl.when(i != 0)
        def _():
            remote(tg.at[cols], tgr.at[x * 2 + c], 1, ((pair & 56) | (px << 1) | zh, tok)).start()

        @pl.when(jnp.logical_and(i == 0, c != zh))
        def _():
            remote(tg.at[cols], tgr.at[x * 2 + c], 1, (pair ^ 1, tok)).start()

        @pl.when(jnp.logical_and(i == 0, c == zh))
        def _():
            tgr[x * 2 + c] = tg[cols]

        return 0

    lax.fori_loop(0, 4, send_targets, 0)
    place_maps(1, lo, hi, onehot, inv)
    whole(v0.at[:, pl.ds(0, 96)], 0).wait_recv()

    def send_blocks(j, h):
        def send_block(k, _):
            i = k >> 3
            m = k & 7
            to = pair ^ ((i << 1) | ((m & 6) << 3) | (m & 1))
            rows = pl.ds(pl.multiple_of((((to >> 4) << 1) | (to & 1)) * RB, RB), RB)
            block = part.at[j, h, x ^ i, rows]
            remote(block, arrived.at[j, h, i, m], 9 + (j * 2 + h) * 4 + i, (to, tok)).start()
            return 0

        lax.fori_loop(1, 32, send_block, 0)
        arrived[j, h, 0, 0] = part[j, h, x, my_rows, :]
        for i in range(4):
            leaving.append((arrived.at[j, h, i, pl.ds(0 if i else 1, 8 if i else 7)], 9 + (j * 2 + h) * 4 + i))

    my_rows = pl.ds(pl.multiple_of(((y << 1) | c) * RB, RB), RB)
    for j in range(2):
        vp[...] = v0[j].astype(F32)

        def spread(g, _):
            rows = pl.ds(pl.multiple_of(g * 16, 16), 16)
            values = jnp.concatenate([vp[pl.ds(g * 16 + b, 8, stride=2), :] for b in range(2)], 0)
            for h in range(16):
                place = inv[j, h, rows, :]
                chosen = jnp.take_along_axis(values, jnp.maximum(place - 1, 0), axis=1)
                dense[rows, h * 128:h * 128 + 128] = jnp.where(place > 0, chosen, 0.0).astype(BF16)
            return 0

        lax.fori_loop(0, 8, spread, 0)
        dec_copy[j].wait()
        for px in range(4):
            both = jnp.dot(dense[...], dec[j, :, px * CB:px * CB + CB], preferred_element_type=F32)
            part[j, 0, px] = both[:, :HB]
            part[j, 1, px] = both[:, HB:]
        send_blocks(j, 0)

    send_blocks(0, 1)
    send_blocks(1, 1)

    def turn(j):
        def block(f, _):
            cols = pl.ds(pl.multiple_of(f * 256, 256), 256)
            dect[j, :, cols] = dec[j, cols, :].T
            return 0

        lax.fori_loop(0, 8, block, 0)

    sums[...] = jnp.zeros((2, L, RB, HB), F32)

    @pl.when(c == zh)
    def _():
        whole(tgr.at[pl.ds(0, 7)], 1).wait_recv()
        for l in range(L):
            for b in range(2):
                for h in range(2):
                    sums[h, l, b * 8:b * 8 + 8, :] = -tgr.reshape(8 * 48, 128)[
                        pl.ds(h * 24 + l * 2 + b, 8, stride=48), :]

    turn(0)
    exchange = [remote(sums.at[h], sums_z.at[h], 2 if h else 7, (pair ^ 8, tok)) for h in range(2)]

    def add_up(h):
        for j in range(2):
            for i in range(4):
                whole(arrived.at[j, h, i, pl.ds(0 if i else 1, 8 if i else 7)],
                      9 + (j * 2 + h) * 4 + i).wait_recv()

                def add(m, totals):
                    source = pair ^ ((i << 1) | ((m & 6) << 3) | (m & 1))
                    target = sp[1, 2 * source + j]
                    block = arrived[j, h, i, m]
                    return tuple(t + jnp.where(target == l, block, 0.0) for l, t in enumerate(totals))

                totals = lax.fori_loop(0, 8, add, tuple(sums[h, l] for l in range(L)), unroll=2)
                for l in range(L):
                    sums[h, l] = totals[l]
        exchange[h].start()

    def give_back(h):
        exchange[h].wait()
        for l in range(L):
            resid[h, l] = ((sums[h, l] + sums_z[h, l]) * D ** (-0.5)).astype(BF16)
        my_cols = pl.ds(pl.multiple_of(x * CB + h * HB, HB), HB)
        for j in range(2):
            def give(k, _):
                to = mate(k)
                back[j, k, h] = resid[h, jnp.maximum(sp[1, 2 * to + j], 0)]
                remote(back.at[j, k, h], grad_in.at[j, my_rows, my_cols], 3 + j, (to, tok)).start()
                return 0

            lax.fori_loop(1, 32, give, 0)
            grad_in[j, my_rows, my_cols] = resid[h, jnp.maximum(sp[1, 2 * pair + j], 0)]

    def sent_targets():
        @pl.when(c == zh)
        def _():
            whole(tgr.at[pl.ds(0, 3)], 1).wait_send()

        @pl.when(c != zh)
        def _():
            whole(tgr.at[pl.ds(0, 4)], 1).wait_send()

    add_up(0)
    add_up(1)
    give_back(0)
    turn(1)
    sent_targets()
    give_back(1)
    for j in range(2):
        leaving.append((back.at[j, pl.ds(1, 31)], 3 + j))

    for j in range(2):
        whole(back.at[j, pl.ds(1, 31)], 3 + j).wait_recv()
        picked[...] = jnp.zeros((ROWS, K), F32)

        def features(f, _):
            grads = jnp.dot(grad_in[j], dect[j, :, pl.ds(pl.multiple_of(f * 256, 256), 256)],
                            preferred_element_type=F32)
            for q in range(2):
                chosen = jnp.take_along_axis(grads[:, q * 128:q * 128 + 128], lo[j], axis=1)
                picked[...] = jnp.where(hi[j] == f * 2 + q, chosen, picked[...])
            return 0

        lax.fori_loop(0, 8, features, 0, unroll=4)
        for gb in range(16):
            start = (gb // 4) * 64 + j * 4 + gb % 4
            gsend.reshape(256, K)[pl.ds(start, 8, stride=8), :] = picked[gb * 8:gb * 8 + 8, :]

    def send_picked(k, _):
        to = mate(k)
        q = ((to >> 4) << 3) | (to & 7)
        remote(gsend.at[q], grecv.at[k], 5, (to, tok)).start()
        return 0

    lax.fori_loop(1, 32, send_picked, 0)
    grecv[0] = gsend[(y << 3) | (x << 1) | c]
    leaving.append((grecv.at[pl.ds(1, 31)], 5))
    whole(grecv.at[pl.ds(1, 31)], 5).wait_recv()

    def add_picked(k, totals):
        first = 2 * mate(k)
        upper = lax.broadcasted_iota(I32, (8, K), 0) < 4
        source = jnp.where(upper, sp[0, first], sp[0, first + 1])
        block = grecv[k]
        return tuple(t + jnp.where(source == l, block, 0.0) for l, t in enumerate(totals))

    totals = lax.fori_loop(0, 32, add_picked, tuple(jnp.zeros((8, K), F32) for _ in range(L)), unroll=2)
    for l in range(L):
        both = totals[l][0:4] + totals[l][4:8]
        fin[0, 2 * l:2 * l + 2, :] = both[0:2]
        fin[1, 2 * l:2 * l + 2, :] = both[2:4]
    for z in range(2):
        fin[z, 22:24, :] = jnp.zeros((2, K), F32)

    me = (zh << 2) | tok

    def send_final(m, _):
        remote(fin.at[zh ^ (m >> 2)], fin_r.at[me], 6, (pair ^ ((m & 4) << 1), tok ^ (m & 3))).start()
        return 0

    lax.fori_loop(1, 8, send_final, 0)
    fin_r[me] = fin[zh]
    whole(fin_r.at[pl.ds(0, 7)], 6).wait_recv()
    leaving.append((fin_r.at[pl.ds(0, 7)], 6))
    total = fin_r[0]
    for m in range(1, 8):
        total = total + fin_r[m]
    for l in range(L):
        out[l] = total[2 * l:2 * l + 2]
    finish()


def local(act_vals, act_idx, slot_pairs, decoders, targets):
    hbm, vmem = pl.BlockSpec(memory_space=pltpu.HBM), pl.BlockSpec(memory_space=pltpu.VMEM)
    return pl.pallas_call(
        kernel,
        out_shape=jax.ShapeDtypeStruct((L, 2, K), F32),
        in_specs=[hbm] * 5,
        out_specs=vmem,
        scratch_shapes=[
            pltpu.SMEM((2, 128), I32),
            pltpu.VMEM((L, 32, K), BF16),
            pltpu.VMEM((L, ROWS, K), I32),
            pltpu.VMEM((L, 2, DC), BF16),
            pltpu.VMEM((2, F, DC), BF16),
            pltpu.VMEM((2, ROWS, K), BF16),
            pltpu.VMEM((ROWS, K), I32),
            pltpu.VMEM((ROWS, K), F32),
            pltpu.VMEM((2, ROWS, K), I32),
            pltpu.VMEM((2, ROWS, K), I32),
            pltpu.VMEM((ROWS * 16, K), F32),
            pltpu.VMEM((2, 16, ROWS, K), I32),
            pltpu.VMEM((ROWS, F), BF16),
            pltpu.VMEM((2, DC, F), BF16),
            pltpu.VMEM((2, 2, 4, ROWS, HB), F32),
            pltpu.VMEM((2, 2, 4, 8, RB, HB), F32),
            pltpu.VMEM((8, 24, 128), F32),
            pltpu.VMEM((8, 2, 24, 128), F32),
            pltpu.VMEM((2, L, RB, HB), F32),
            pltpu.VMEM((2, L, RB, HB), F32),
            pltpu.VMEM((2, L, RB, HB), BF16),
            pltpu.VMEM((2, 32, 2, RB, HB), BF16),
            pltpu.VMEM((2, ROWS, DC), BF16),
            pltpu.VMEM((ROWS, K), F32),
            pltpu.VMEM((32, 8, K), F32),
            pltpu.VMEM((32, 8, K), F32),
            pltpu.VMEM((2, 24, K), F32),
            pltpu.VMEM((8, 24, K), F32),
            pltpu.SemaphoreType.DMA((6,)),
            pltpu.SemaphoreType.DMA((25,)),
            pltpu.SemaphoreType.DMA((25,)),
        ],
        compiler_params=pltpu.CompilerParams(collective_id=0, has_side_effects=True, vmem_limit_bytes=60 << 20),
        cost_estimate=pl.CostEstimate(flops=2 * 2 * 2 * ROWS * F * DC, bytes_accessed=10 << 20, transcendentals=0),
        name="transcoder",
    )(slot_pairs.T, act_vals, act_idx, decoders, targets)


def solution(mesh):
    return jax.shard_map(
        local,
        mesh=mesh,
        in_specs=(P(None, "tok", None), P(), P(), P("pair", None, "tok"), P(None, "pair", "tok")),
        out_specs=P(None, "pair", None),
        check_vma=False,
    )
```

```python
import functools

import jax
import jax.numpy as jnp
from jax import lax
from jax.experimental import pallas as pl
from jax.experimental.pallas import tpu as pltpu
from jax.sharding import PartitionSpec as P

MESH = pl.DeviceIdType.MESH
F32, BF16, I32 = jnp.float32, jnp.bfloat16, jnp.int32
NT = (((1,), (1,)), ((), ()))
L, K, F, D = 11, 128, 2048, 4096
DC = 1024
ROWS = 128
CB = 256
HB = 128
RB = 16
UNROLL = 16


def place_maps(j, lo, hi, onehot, inv):
    nothing = jnp.zeros((16, K), BF16)
    lows = lax.broadcasted_iota(I32, (128, K), 0).astype(F32).astype(BF16)
    highs = lax.broadcasted_iota(I32, (16, K), 0)
    places = lax.broadcasted_iota(I32, (16, K), 1) + 1

    def masks(r):
        low = jnp.broadcast_to(lo[j, pl.ds(r, 1), :].astype(F32).astype(BF16), (128, K))
        high = jnp.broadcast_to(hi[j, pl.ds(r, 1), :], (16, K))
        return (jnp.where(high == highs, places, 0).astype(F32).astype(BF16),
                jnp.where(low == lows, jnp.ones((), BF16), jnp.zeros((), BF16)))

    def rows(i, _):
        for u in range(UNROLL):
            r = i * (2 * UNROLL) + 2 * u
            (left0, right0), (left1, right1) = masks(r), masks(r + 1)
            left = jnp.concatenate([jnp.concatenate([left0, nothing], 1), jnp.concatenate([nothing, left1], 1)], 0)
            onehot[pl.ds(pl.multiple_of(r * 16, 32), 32), :] = lax.dot_general(
                left, jnp.concatenate([right0, right1], 1), NT, preferred_element_type=F32)
        return 0

    lax.fori_loop(0, 64 // UNROLL, rows, 0)
    for h in range(16):
        inv[j, h] = onehot[pl.ds(h, ROWS, stride=16), :].astype(I32)


def kernel(sp_hbm, vals_hbm, idx_hbm, dec_hbm, tg_hbm, out, sp, vals, idx, tg_ref, dec, v0, i0, vp, lo, hi, onehot, inv,
           dense, dect, part, arrived, tg, tgr, sums, sums_z, resid, back, grad_in, picked, gsend, grecv, fin, fin_r,
           loc_sem, send_sem, recv_sem):
    pair, tok = lax.axis_index("pair"), lax.axis_index("tok")
    y, zh, x, c = pair >> 4, (pair >> 3) & 1, (pair >> 1) & 3, pair & 1

    def mate(k):
        bits = (k * 5) & 31
        return pair ^ (((bits & 24) << 1) | (bits & 7))

    def remote(src, dst, n, device):
        return pltpu.make_async_remote_copy(src_ref=src, dst_ref=dst, send_sem=send_sem.at[n],
                                            recv_sem=recv_sem.at[n], device_id=device, device_id_type=MESH)

    def whole(ref, n):
        return remote(ref, ref, n, (pair ^ 1, tok))

    leaving = []

    def finish():
        for ref, n in leaving:
            whole(ref, n).wait_send()

    sp_copy = pltpu.make_async_copy(sp_hbm, sp, loc_sem.at[2])
    vals_copy = pltpu.make_async_copy(vals_hbm, vals, loc_sem.at[3])
    idx_copy = pltpu.make_async_copy(idx_hbm, idx, loc_sem.at[4])
    tg_copy = pltpu.make_async_copy(tg_hbm, tg_ref, loc_sem.at[5])
    dec_copy = [pltpu.make_async_copy(dec_hbm.at[j], dec.at[j], loc_sem.at[j]) for j in range(2)]
    sp_copy.start()
    vals_copy.start()
    idx_copy.start()
    tg_copy.start()
    dec_copy[0].start()
    dec_copy[1].start()

    barrier = pltpu.get_barrier_semaphore()

    def greet_column(m, _):
        pl.semaphore_signal(barrier, inc=1, device_id=(pair ^ ((m & 4) << 1), tok ^ (m & 3)), device_id_type=MESH)
        return 0

    lax.fori_loop(1, 8, greet_column, 0)

    def greet(k, _):
        pl.semaphore_signal(barrier, inc=1, device_id=(mate(k), tok), device_id_type=MESH)
        return 0

    lax.fori_loop(1, 32, greet, 0)

    sp_copy.wait()
    idx_copy.wait()
    for j in range(2):
        i0[...] = idx[jnp.maximum(sp[0, 2 * pair + j], 0)]
        for gb in range(16):
            rows = i0[pl.ds((gb // 2) * 16 + gb % 2, 8, stride=2), :]
            lo[j, gb * 8:gb * 8 + 8, :] = jnp.bitwise_and(rows, 127)
            hi[j, gb * 8:gb * 8 + 8, :] = lax.shift_right_logical(rows, 7)

    place_maps(0, lo, hi, onehot, inv)

    tg_copy.wait()
    for b in range(8):
        for l in range(L):
            tg[b, 2 * l:2 * l + 2, :] = tg_ref[l, :, b * 128:b * 128 + 128].astype(F32)
        tg[b, 22:24, :] = jnp.zeros((2, 128), F32)
    mine = pl.ds(pl.multiple_of(tok * 32, 32), 32)
    vals_copy.wait()
    for j in range(2):
        v0[j, mine, :] = vals[jnp.maximum(sp[0, 2 * pair + j], 0)]

    pl.semaphore_wait(barrier, 38)

    for d in range(1, 4):
        remote(v0.at[:, mine], v0.at[:, mine], 0, (pair, tok ^ d)).start()
    leaving.append((v0.at[:, pl.ds(0, 96)], 0))

    def send_targets(i, _):
        px = x ^ i
        cols = pl.ds(px * 2, 2)

        @pl.when(i != 0)
        def _():
            remote(tg.at[cols], tgr.at[x * 2 + c], 1, ((pair & 56) | (px << 1) | zh, tok)).start()

        @pl.when(jnp.logical_and(i == 0, c != zh))
        def _():
            remote(tg.at[cols], tgr.at[x * 2 + c], 1, (pair ^ 1, tok)).start()

        @pl.when(jnp.logical_and(i == 0, c == zh))
        def _():
            tgr[x * 2 + c] = tg[cols]

        return 0

    lax.fori_loop(0, 4, send_targets, 0)

    def group(j, h, i):
        return arrived.at[j, h, pl.ds(i * 8 if i else 1, 8 if i else 7)]

    def send_blocks(j, h):
        def send_block(k, _):
            to = mate(k)
            rows = pl.ds(pl.multiple_of((((to >> 4) << 1) | (to & 1)) * RB, RB), RB)
            block = part.at[j, h, (to >> 1) & 3, rows]
            remote(block, arrived.at[j, h, k], 9 + (j * 2 + h) * 4 + (k >> 3), (to, tok)).start()
            return 0

        lax.fori_loop(1, 32, send_block, 0)
        arrived[j, h, 0] = part[j, h, x, my_rows, :]
        for i in range(4):
            leaving.append((group(j, h, i), 9 + (j * 2 + h) * 4 + i))

    my_rows = pl.ds(pl.multiple_of(((y << 1) | c) * RB, RB), RB)
    for j in range(2):
        if j == 0:
            place_maps(1, lo, hi, onehot, inv)
            whole(v0.at[:, pl.ds(0, 96)], 0).wait_recv()
        vp[...] = v0[j].astype(F32)

        def spread(g, _):
            rows = pl.ds(pl.multiple_of(g * 16, 16), 16)
            values = jnp.concatenate([vp[pl.ds(g * 16 + b, 8, stride=2), :] for b in range(2)], 0)
            for h in range(16):
                place = inv[j, h, rows, :]
                chosen = jnp.take_along_axis(values, jnp.maximum(place - 1, 0), axis=1)
                dense[rows, h * 128:h * 128 + 128] = jnp.where(place > 0, chosen, 0.0).astype(BF16)
            return 0

        lax.fori_loop(0, 8, spread, 0)
        dec_copy[j].wait()
        for px in range(4):
            both = jnp.dot(dense[...], dec[j, :, px * CB:px * CB + CB], preferred_element_type=F32)
            part[j, 0, px] = both[:, :HB]
            part[j, 1, px] = both[:, HB:]
        send_blocks(j, 0)
    send_blocks(0, 1)
    send_blocks(1, 1)

    def turn(j):
        def block(f, _):
            cols = pl.ds(pl.multiple_of(f * 256, 256), 256)
            dect[j, :, cols] = dec[j, cols, :].T
            return 0

        lax.fori_loop(0, 8, block, 0)

    sums[...] = jnp.zeros((2, L, RB, HB), F32)

    @pl.when(c == zh)
    def _():
        whole(tgr.at[pl.ds(0, 7)], 1).wait_recv()
        for l in range(L):
            for b in range(2):
                for h in range(2):
                    sums[h, l, b * 8:b * 8 + 8, :] = -tgr.reshape(8 * 48, 128)[
                        pl.ds(h * 24 + l * 2 + b, 8, stride=48), :]

    turn(0)
    zsem = (7, 2)

    def add_up(h):
        for j in range(2):
            for i in range(4):
                whole(group(j, h, i), 9 + (j * 2 + h) * 4 + i).wait_recv()

                def add(m, totals):
                    target = sp[1, 2 * mate(i * 8 + m) + j]
                    block = arrived[j, h, i * 8 + m]
                    return tuple(t + jnp.where(target == l, block, 0.0) for l, t in enumerate(totals))

                totals = lax.fori_loop(0, 8, add, tuple(sums[h, l] for l in range(L)), unroll=2)
                for l in range(L):
                    sums[h, l] = totals[l]

        def send_layer(l, _):
            remote(sums.at[h, l], sums_z.at[h, l], zsem[h], (pair ^ 8, tok)).start()
            return 0

        lax.fori_loop(0, L, send_layer, 0)
        leaving.append((sums.at[h], zsem[h]))

    def give_back(h):
        whole(sums_z.at[h], zsem[h]).wait_recv()
        for l in range(L):
            resid[h, l] = ((sums[h, l] + sums_z[h, l]) * D ** (-0.5)).astype(BF16)
        my_cols = pl.ds(pl.multiple_of(x * CB + h * HB, HB), HB)
        for j in range(2):
            def give(k, _):
                to = mate(k)
                back[j, k, h] = resid[h, jnp.maximum(sp[1, 2 * to + j], 0)]
                remote(back.at[j, k, h], grad_in.at[j, my_rows, my_cols], 3 + j, (to, tok)).start()
                return 0

            lax.fori_loop(1, 32, give, 0)
            grad_in[j, my_rows, my_cols] = resid[h, jnp.maximum(sp[1, 2 * pair + j], 0)]

    def sent_targets():
        @pl.when(c == zh)
        def _():
            whole(tgr.at[pl.ds(0, 3)], 1).wait_send()

        @pl.when(c != zh)
        def _():
            whole(tgr.at[pl.ds(0, 4)], 1).wait_send()

    add_up(0)
    add_up(1)
    give_back(0)
    turn(1)
    sent_targets()
    give_back(1)
    for j in range(2):
        leaving.append((back.at[j, pl.ds(1, 31)], 3 + j))

    for j in range(2):
        whole(back.at[j, pl.ds(1, 31)], 3 + j).wait_recv()
        picked[...] = jnp.zeros((ROWS, K), F32)

        def features(f, _):
            grads = jnp.dot(grad_in[j], dect[j, :, pl.ds(pl.multiple_of(f * 256, 256), 256)],
                            preferred_element_type=F32)
            for q in range(2):
                chosen = jnp.take_along_axis(grads[:, q * 128:q * 128 + 128], lo[j], axis=1)
                picked[...] = jnp.where(hi[j] == f * 2 + q, chosen, picked[...])
            return 0

        lax.fori_loop(0, 8, features, 0, unroll=4)
        for gb in range(16):
            start = (gb // 4) * 64 + j * 4 + gb % 4
            gsend.reshape(256, K)[pl.ds(start, 8, stride=8), :] = picked[gb * 8:gb * 8 + 8, :]

    def send_picked(k, _):
        to = mate(k)
        q = ((to >> 4) << 3) | (to & 7)
        remote(gsend.at[q], grecv.at[k], 5, (to, tok)).start()
        return 0

    lax.fori_loop(1, 32, send_picked, 0)
    grecv[0] = gsend[(y << 3) | (x << 1) | c]
    leaving.append((grecv.at[pl.ds(1, 31)], 5))
    whole(grecv.at[pl.ds(1, 31)], 5).wait_recv()

    def add_picked(k, totals):
        first = 2 * mate(k)
        upper = lax.broadcasted_iota(I32, (8, K), 0) < 4
        source = jnp.where(upper, sp[0, first], sp[0, first + 1])
        block = grecv[k]
        return tuple(t + jnp.where(source == l, block, 0.0) for l, t in enumerate(totals))

    totals = lax.fori_loop(0, 32, add_picked, tuple(jnp.zeros((8, K), F32) for _ in range(L)), unroll=2)
    for l in range(L):
        both = totals[l][0:4] + totals[l][4:8]
        fin[0, 2 * l:2 * l + 2, :] = both[0:2]
        fin[1, 2 * l:2 * l + 2, :] = both[2:4]
    for z in range(2):
        fin[z, 22:24, :] = jnp.zeros((2, K), F32)

    me = (zh << 2) | tok

    def send_final(m, _):
        remote(fin.at[zh ^ (m >> 2)], fin_r.at[me], 6, (pair ^ ((m & 4) << 1), tok ^ (m & 3))).start()
        return 0

    lax.fori_loop(1, 8, send_final, 0)
    fin_r[me] = fin[zh]
    whole(fin_r.at[pl.ds(0, 7)], 6).wait_recv()
    leaving.append((fin_r.at[pl.ds(0, 7)], 6))
    total = fin_r[0]
    for m in range(1, 8):
        total = total + fin_r[m]
    for l in range(L):
        out[l] = total[2 * l:2 * l + 2]
    finish()


def local(act_vals, act_idx, slot_pairs, decoders, targets):
    hbm, vmem = pl.BlockSpec(memory_space=pltpu.HBM), pl.BlockSpec(memory_space=pltpu.VMEM)
    return pl.pallas_call(
        kernel,
        out_shape=jax.ShapeDtypeStruct((L, 2, K), F32),
        in_specs=[hbm] * 5,
        out_specs=vmem,
        scratch_shapes=[
            pltpu.SMEM((2, 128), I32),
            pltpu.VMEM((L, 32, K), BF16),
            pltpu.VMEM((L, ROWS, K), I32),
            pltpu.VMEM((L, 2, DC), BF16),
            pltpu.VMEM((2, F, DC), BF16),
            pltpu.VMEM((2, ROWS, K), BF16),
            pltpu.VMEM((ROWS, K), I32),
            pltpu.VMEM((ROWS, K), F32),
            pltpu.VMEM((2, ROWS, K), I32),
            pltpu.VMEM((2, ROWS, K), I32),
            pltpu.VMEM((ROWS * 16, K), F32),
            pltpu.VMEM((2, 16, ROWS, K), I32),
            pltpu.VMEM((ROWS, F), BF16),
            pltpu.VMEM((2, DC, F), BF16),
            pltpu.VMEM((2, 2, 4, ROWS, HB), F32),
            pltpu.VMEM((2, 2, 32, RB, HB), F32),
            pltpu.VMEM((8, 24, 128), F32),
            pltpu.VMEM((8, 2, 24, 128), F32),
            pltpu.VMEM((2, L, RB, HB), F32),
            pltpu.VMEM((2, L, RB, HB), F32),
            pltpu.VMEM((2, L, RB, HB), BF16),
            pltpu.VMEM((2, 32, 2, RB, HB), BF16),
            pltpu.VMEM((2, ROWS, DC), BF16),
            pltpu.VMEM((ROWS, K), F32),
            pltpu.VMEM((32, 8, K), F32),
            pltpu.VMEM((32, 8, K), F32),
            pltpu.VMEM((2, 24, K), F32),
            pltpu.VMEM((8, 24, K), F32),
            pltpu.SemaphoreType.DMA((6,)),
            pltpu.SemaphoreType.DMA((25,)),
            pltpu.SemaphoreType.DMA((25,)),
        ],
        compiler_params=pltpu.CompilerParams(collective_id=0, has_side_effects=True, vmem_limit_bytes=60 << 20),
        cost_estimate=pl.CostEstimate(flops=2 * 2 * 2 * ROWS * F * DC, bytes_accessed=10 << 20, transcendentals=0),
        name="transcoder",
    )(slot_pairs.T, act_vals, act_idx, decoders, targets)


def solution(mesh):
    return jax.shard_map(
        local,
        mesh=mesh,
        in_specs=(P(None, "tok", None), P(), P(), P("pair", None, "tok"), P(None, "pair", "tok")),
        out_specs=P(None, "pair", None),
        check_vma=False,
    )
```

```python
import functools

import jax
import jax.numpy as jnp
from jax import lax
from jax.experimental import pallas as pl
from jax.experimental.pallas import tpu as pltpu
from jax.sharding import PartitionSpec as P

MESH = pl.DeviceIdType.MESH
F32, BF16, I32 = jnp.float32, jnp.bfloat16, jnp.int32
NT = (((1,), (1,)), ((), ()))
L, K, F, D = 11, 128, 2048, 4096
DC = 1024
ROWS = 128
CB = 256
HB = 128
RB = 16
UNROLL = 32
EARLY = 8


def place_maps(j, lo, hi, onehot, inv):
    nothing = jnp.zeros((16, K), BF16)
    lows = lax.broadcasted_iota(I32, (128, K), 0).astype(F32).astype(BF16)
    highs = lax.broadcasted_iota(I32, (16, K), 0)
    places = lax.broadcasted_iota(I32, (16, K), 1) + 1

    def masks(r):
        low = jnp.broadcast_to(lo[j, pl.ds(r, 1), :].astype(F32).astype(BF16), (128, K))
        high = jnp.broadcast_to(hi[j, pl.ds(r, 1), :], (16, K))
        return (jnp.where(high == highs, places, 0).astype(F32).astype(BF16),
                jnp.where(low == lows, jnp.ones((), BF16), jnp.zeros((), BF16)))

    def rows(i, _):
        for u in range(UNROLL):
            r = i * (2 * UNROLL) + 2 * u
            (left0, right0), (left1, right1) = masks(r), masks(r + 1)
            left = jnp.concatenate([jnp.concatenate([left0, nothing], 1), jnp.concatenate([nothing, left1], 1)], 0)
            onehot[pl.ds(pl.multiple_of(r * 16, 32), 32), :] = lax.dot_general(
                left, jnp.concatenate([right0, right1], 1), NT, preferred_element_type=F32)
        return 0

    lax.fori_loop(0, 64 // UNROLL, rows, 0)
    for h in range(16):
        inv[j, h] = onehot[pl.ds(h, ROWS, stride=16), :].astype(I32)


def kernel(sp_hbm, vals_hbm, idx_hbm, dec_hbm, tg_hbm, out, sp, vals, idx, tg_ref, dec, v0, i0, vp, lo, hi, onehot, inv,
           dense, dect, part, arrived, tg, tgr, sums, sums_z, resid, back, grad_in, picked, gsend, grecv, fin, fin_r,
           loc_sem, send_sem, recv_sem):
    pair, tok = lax.axis_index("pair"), lax.axis_index("tok")
    y, zh, x, c = pair >> 4, (pair >> 3) & 1, (pair >> 1) & 3, pair & 1

    def mate(k):
        bits = (k * 5) & 31
        return pair ^ (((bits & 24) << 1) | (bits & 7))

    def remote(src, dst, n, device):
        return pltpu.make_async_remote_copy(src_ref=src, dst_ref=dst, send_sem=send_sem.at[n],
                                            recv_sem=recv_sem.at[n], device_id=device, device_id_type=MESH)

    def whole(ref, n):
        return remote(ref, ref, n, (pair ^ 1, tok))

    leaving = []

    def finish():
        for ref, n in leaving:
            whole(ref, n).wait_send()

    sp_copy = pltpu.make_async_copy(sp_hbm, sp, loc_sem.at[2])
    vals_copy = pltpu.make_async_copy(vals_hbm, vals, loc_sem.at[3])
    idx_copy = pltpu.make_async_copy(idx_hbm, idx, loc_sem.at[4])
    tg_copy = pltpu.make_async_copy(tg_hbm, tg_ref, loc_sem.at[5])
    dec_copy = [pltpu.make_async_copy(dec_hbm.at[j], dec.at[j], loc_sem.at[j]) for j in range(2)]
    sp_copy.start()
    vals_copy.start()
    idx_copy.start()
    tg_copy.start()
    dec_copy[0].start()
    dec_copy[1].start()

    barrier = pltpu.get_barrier_semaphore()

    def greet_column(m, _):
        pl.semaphore_signal(barrier, inc=1, device_id=(pair ^ ((m & 4) << 1), tok ^ (m & 3)), device_id_type=MESH)
        return 0

    lax.fori_loop(1, 8, greet_column, 0)

    def greet(k, _):
        pl.semaphore_signal(barrier, inc=1, device_id=(mate(k), tok), device_id_type=MESH)
        return 0

    lax.fori_loop(1, 32, greet, 0)

    sp_copy.wait()
    idx_copy.wait()
    for j in range(2):
        i0[...] = idx[jnp.maximum(sp[0, 2 * pair + j], 0)]
        for gb in range(16):
            rows = i0[pl.ds((gb // 2) * 16 + gb % 2, 8, stride=2), :]
            lo[j, gb * 8:gb * 8 + 8, :] = jnp.bitwise_and(rows, 127)
            hi[j, gb * 8:gb * 8 + 8, :] = lax.shift_right_logical(rows, 7)

    place_maps(0, lo, hi, onehot, inv)

    tg_copy.wait()
    for b in range(8):
        for l in range(L):
            tg[b, 2 * l:2 * l + 2, :] = tg_ref[l, :, b * 128:b * 128 + 128].astype(F32)
        tg[b, 22:24, :] = jnp.zeros((2, 128), F32)
    mine = pl.ds(pl.multiple_of(tok * 32, 32), 32)
    vals_copy.wait()
    for j in range(2):
        v0[j, mine, :] = vals[jnp.maximum(sp[0, 2 * pair + j], 0)]

    pl.semaphore_wait(barrier, 38)

    for d in range(1, 4):
        remote(v0.at[:, mine], v0.at[:, mine], 0, (pair, tok ^ d)).start()
    leaving.append((v0.at[:, pl.ds(0, 96)], 0))

    def send_targets(i, _):
        px = x ^ i
        cols = pl.ds(px * 2, 2)

        @pl.when(i != 0)
        def _():
            remote(tg.at[cols], tgr.at[x * 2 + c], 1, ((pair & 56) | (px << 1) | zh, tok)).start()

        @pl.when(jnp.logical_and(i == 0, c != zh))
        def _():
            remote(tg.at[cols], tgr.at[x * 2 + c], 1, (pair ^ 1, tok)).start()

        @pl.when(jnp.logical_and(i == 0, c == zh))
        def _():
            tgr[x * 2 + c] = tg[cols]

        return 0

    lax.fori_loop(0, 4, send_targets, 0)

    def group(j, h, i):
        return arrived.at[j, h, pl.ds(i * 8 if i else 1, 8 if i else 7)]

    def send_blocks(j, h, first=1, end=32):
        def send_block(k, _):
            to = mate(k)
            rows = pl.ds(pl.multiple_of((((to >> 4) << 1) | (to & 1)) * RB, RB), RB)
            block = part.at[j, h, (to >> 1) & 3, rows]
            remote(block, arrived.at[j, h, k], 9 + (j * 2 + h) * 4 + (k >> 3), (to, tok)).start()
            return 0

        lax.fori_loop(first, end, send_block, 0, unroll=4)
        if end < 32:
            return
        arrived[j, h, 0] = part[j, h, x, my_rows, :]
        for i in range(4):
            leaving.append((group(j, h, i), 9 + (j * 2 + h) * 4 + i))

    my_rows = pl.ds(pl.multiple_of(((y << 1) | c) * RB, RB), RB)
    for j in range(2):
        if j == 0:
            place_maps(1, lo, hi, onehot, inv)
            whole(v0.at[:, pl.ds(0, 96)], 0).wait_recv()
        vp[...] = v0[j].astype(F32)

        def spread(g, _):
            rows = pl.ds(pl.multiple_of(g * 16, 16), 16)
            values = jnp.concatenate([vp[pl.ds(g * 16 + b, 8, stride=2), :] for b in range(2)], 0)
            for h in range(16):
                place = inv[j, h, rows, :]
                chosen = jnp.take_along_axis(values, jnp.maximum(place - 1, 0), axis=1)
                dense[rows, h * 128:h * 128 + 128] = jnp.where(place > 0, chosen, 0.0).astype(BF16)
            return 0

        lax.fori_loop(0, 8, spread, 0, unroll=4)
        dec_copy[j].wait()
        for px in range(4):
            both = jnp.dot(dense[...], dec[j, :, px * CB:px * CB + CB], preferred_element_type=F32)
            part[j, 0, px] = both[:, :HB]
            part[j, 1, px] = both[:, HB:]
        send_blocks(j, 0)
        if j == 0:
            send_blocks(0, 1, 1, EARLY)
    send_blocks(0, 1, EARLY)
    send_blocks(1, 1)

    def turn(j):
        def block(f, _):
            cols = pl.ds(pl.multiple_of(f * 256, 256), 256)
            dect[j, :, cols] = dec[j, cols, :].T
            return 0

        lax.fori_loop(0, 8, block, 0)

    sums[...] = jnp.zeros((2, L, RB, HB), F32)

    @pl.when(c == zh)
    def _():
        whole(tgr.at[pl.ds(0, 7)], 1).wait_recv()
        for l in range(L):
            for b in range(2):
                for h in range(2):
                    sums[h, l, b * 8:b * 8 + 8, :] = -tgr.reshape(8 * 48, 128)[
                        pl.ds(h * 24 + l * 2 + b, 8, stride=48), :]

    turn(0)
    zsem = (7, 2)

    def add_up(h):
        for j in range(2):
            for i in range(4):
                whole(group(j, h, i), 9 + (j * 2 + h) * 4 + i).wait_recv()

                def add(m, totals):
                    target = sp[1, 2 * mate(i * 8 + m) + j]
                    block = arrived[j, h, i * 8 + m]
                    return tuple(t + jnp.where(target == l, block, 0.0) for l, t in enumerate(totals))

                totals = lax.fori_loop(0, 8, add, tuple(sums[h, l] for l in range(L)), unroll=2)
                for l in range(L):
                    sums[h, l] = totals[l]

        def send_layer(l, _):
            remote(sums.at[h, l], sums_z.at[h, l], zsem[h], (pair ^ 8, tok)).start()
            return 0

        lax.fori_loop(0, L, send_layer, 0)
        leaving.append((sums.at[h], zsem[h]))

    def give_back(h):
        whole(sums_z.at[h], zsem[h]).wait_recv()
        for l in range(L):
            resid[h, l] = ((sums[h, l] + sums_z[h, l]) * D ** (-0.5)).astype(BF16)
        my_cols = pl.ds(pl.multiple_of(x * CB + h * HB, HB), HB)
        for j in range(2):
            def give(k, _):
                to = mate(k)
                back[j, k, h] = resid[h, jnp.maximum(sp[1, 2 * to + j], 0)]
                remote(back.at[j, k, h], grad_in.at[j, my_rows, my_cols], 3 + j, (to, tok)).start()
                return 0

            lax.fori_loop(1, 32, give, 0, unroll=4)
            grad_in[j, my_rows, my_cols] = resid[h, jnp.maximum(sp[1, 2 * pair + j], 0)]

    def sent_targets():
        @pl.when(c == zh)
        def _():
            whole(tgr.at[pl.ds(0, 3)], 1).wait_send()

        @pl.when(c != zh)
        def _():
            whole(tgr.at[pl.ds(0, 4)], 1).wait_send()

    add_up(0)
    add_up(1)
    give_back(0)
    turn(1)
    sent_targets()
    give_back(1)
    for j in range(2):
        leaving.append((back.at[j, pl.ds(1, 31)], 3 + j))

    for j in range(2):
        whole(back.at[j, pl.ds(1, 31)], 3 + j).wait_recv()
        picked[...] = jnp.zeros((ROWS, K), F32)

        def features(f, _):
            grads = jnp.dot(grad_in[j], dect[j, :, pl.ds(pl.multiple_of(f * 256, 256), 256)],
                            preferred_element_type=F32)
            for q in range(2):
                chosen = jnp.take_along_axis(grads[:, q * 128:q * 128 + 128], lo[j], axis=1)
                picked[...] = jnp.where(hi[j] == f * 2 + q, chosen, picked[...])
            return 0

        lax.fori_loop(0, 8, features, 0, unroll=4)
        for gb in range(16):
            start = (gb // 4) * 64 + j * 4 + gb % 4
            gsend.reshape(256, K)[pl.ds(start, 8, stride=8), :] = picked[gb * 8:gb * 8 + 8, :]

    def send_picked(k, _):
        to = mate(k)
        q = ((to >> 4) << 3) | (to & 7)
        remote(gsend.at[q], grecv.at[k], 5, (to, tok)).start()
        return 0

    lax.fori_loop(1, 32, send_picked, 0, unroll=4)
    grecv[0] = gsend[(y << 3) | (x << 1) | c]
    leaving.append((grecv.at[pl.ds(1, 31)], 5))
    whole(grecv.at[pl.ds(1, 31)], 5).wait_recv()

    def add_picked(k, totals):
        first = 2 * mate(k)
        upper = lax.broadcasted_iota(I32, (8, K), 0) < 4
        source = jnp.where(upper, sp[0, first], sp[0, first + 1])
        block = grecv[k]
        return tuple(t + jnp.where(source == l, block, 0.0) for l, t in enumerate(totals))

    totals = lax.fori_loop(0, 32, add_picked, tuple(jnp.zeros((8, K), F32) for _ in range(L)), unroll=8)
    for l in range(L):
        both = totals[l][0:4] + totals[l][4:8]
        fin[0, 2 * l:2 * l + 2, :] = both[0:2]
        fin[1, 2 * l:2 * l + 2, :] = both[2:4]
    for z in range(2):
        fin[z, 22:24, :] = jnp.zeros((2, K), F32)

    me = (zh << 2) | tok

    def send_final(m, _):
        remote(fin.at[zh ^ (m >> 2)], fin_r.at[me], 6, (pair ^ ((m & 4) << 1), tok ^ (m & 3))).start()
        return 0

    lax.fori_loop(1, 8, send_final, 0)
    fin_r[me] = fin[zh]
    whole(fin_r.at[pl.ds(0, 7)], 6).wait_recv()
    leaving.append((fin_r.at[pl.ds(0, 7)], 6))
    total = fin_r[0]
    for m in range(1, 8):
        total = total + fin_r[m]
    for l in range(L):
        out[l] = total[2 * l:2 * l + 2]
    finish()


def local(act_vals, act_idx, slot_pairs, decoders, targets):
    hbm, vmem = pl.BlockSpec(memory_space=pltpu.HBM), pl.BlockSpec(memory_space=pltpu.VMEM)
    return pl.pallas_call(
        kernel,
        out_shape=jax.ShapeDtypeStruct((L, 2, K), F32),
        in_specs=[hbm] * 5,
        out_specs=vmem,
        scratch_shapes=[
            pltpu.SMEM((2, 128), I32),
            pltpu.VMEM((L, 32, K), BF16),
            pltpu.VMEM((L, ROWS, K), I32),
            pltpu.VMEM((L, 2, DC), BF16),
            pltpu.VMEM((2, F, DC), BF16),
            pltpu.VMEM((2, ROWS, K), BF16),
            pltpu.VMEM((ROWS, K), I32),
            pltpu.VMEM((ROWS, K), F32),
            pltpu.VMEM((2, ROWS, K), I32),
            pltpu.VMEM((2, ROWS, K), I32),
            pltpu.VMEM((ROWS * 16, K), F32),
            pltpu.VMEM((2, 16, ROWS, K), I32),
            pltpu.VMEM((ROWS, F), BF16),
            pltpu.VMEM((2, DC, F), BF16),
            pltpu.VMEM((2, 2, 4, ROWS, HB), F32),
            pltpu.VMEM((2, 2, 32, RB, HB), F32),
            pltpu.VMEM((8, 24, 128), F32),
            pltpu.VMEM((8, 2, 24, 128), F32),
            pltpu.VMEM((2, L, RB, HB), F32),
            pltpu.VMEM((2, L, RB, HB), F32),
            pltpu.VMEM((2, L, RB, HB), BF16),
            pltpu.VMEM((2, 32, 2, RB, HB), BF16),
            pltpu.VMEM((2, ROWS, DC), BF16),
            pltpu.VMEM((ROWS, K), F32),
            pltpu.VMEM((32, 8, K), F32),
            pltpu.VMEM((32, 8, K), F32),
            pltpu.VMEM((2, 24, K), F32),
            pltpu.VMEM((8, 24, K), F32),
            pltpu.SemaphoreType.DMA((6,)),
            pltpu.SemaphoreType.DMA((25,)),
            pltpu.SemaphoreType.DMA((25,)),
        ],
        compiler_params=pltpu.CompilerParams(collective_id=0, has_side_effects=True, vmem_limit_bytes=60 << 20),
        cost_estimate=pl.CostEstimate(flops=2 * 2 * 2 * ROWS * F * DC, bytes_accessed=10 << 20, transcendentals=0),
        name="transcoder",
    )(slot_pairs.T, act_vals, act_idx, decoders, targets)


def solution(mesh):
    return jax.shard_map(
        local,
        mesh=mesh,
        in_specs=(P(None, "tok", None), P(), P(), P("pair", None, "tok"), P(None, "pair", "tok")),
        out_specs=P(None, "pair", None),
        check_vma=False,
    )
```

```python
import functools

import jax
import jax.numpy as jnp
from jax import lax
from jax.experimental import pallas as pl
from jax.experimental.pallas import tpu as pltpu
from jax.sharding import PartitionSpec as P

MESH = pl.DeviceIdType.MESH
F32, BF16, I32 = jnp.float32, jnp.bfloat16, jnp.int32
NT = (((1,), (1,)), ((), ()))
L, K, F, D = 11, 128, 2048, 4096
DC = 1024
ROWS = 128
CB = 256
HB = 128
RB = 16
UNROLL = 32
EARLY = 8


def place_maps(j, lo, hi, onehot, inv):
    nothing = jnp.zeros((16, K), BF16)
    lows = lax.broadcasted_iota(I32, (128, K), 0).astype(F32).astype(BF16)
    highs = lax.broadcasted_iota(I32, (16, K), 0)
    places = lax.broadcasted_iota(I32, (16, K), 1) + 1

    def masks(r):
        low = jnp.broadcast_to(lo[j, pl.ds(r, 1), :].astype(F32).astype(BF16), (128, K))
        high = jnp.broadcast_to(hi[j, pl.ds(r, 1), :], (16, K))
        return (jnp.where(high == highs, places, 0).astype(F32).astype(BF16),
                jnp.where(low == lows, jnp.ones((), BF16), jnp.zeros((), BF16)))

    def rows(i, _):
        for u in range(UNROLL):
            r = i * (2 * UNROLL) + 2 * u
            (left0, right0), (left1, right1) = masks(r), masks(r + 1)
            left = jnp.concatenate([jnp.concatenate([left0, nothing], 1), jnp.concatenate([nothing, left1], 1)], 0)
            onehot[pl.ds(pl.multiple_of(r * 16, 32), 32), :] = lax.dot_general(
                left, jnp.concatenate([right0, right1], 1), NT, preferred_element_type=F32)
        return 0

    lax.fori_loop(0, 64 // UNROLL, rows, 0)
    for h in range(16):
        inv[j, h] = onehot[pl.ds(h, ROWS, stride=16), :].astype(I32)


def kernel(sp_hbm, vals_hbm, idx_hbm, dec_hbm, tg_hbm, out, sp, vals, idx, tg_ref, dec, v0, i0, vp, lo, hi, onehot, inv,
           dense, dect, part, arrived, tg, tgr, sums, sums_z, resid, back, grad_in, picked, gsend, grecv, fin, fin_r,
           loc_sem, send_sem, recv_sem):
    pair, tok = lax.axis_index("pair"), lax.axis_index("tok")
    y, zh, x, c = pair >> 4, (pair >> 3) & 1, (pair >> 1) & 3, pair & 1

    def mate(k):
        bits = (k * 5) & 31
        return pair ^ (((bits & 24) << 1) | (bits & 7))

    def remote(src, dst, n, device):
        return pltpu.make_async_remote_copy(src_ref=src, dst_ref=dst, send_sem=send_sem.at[n],
                                            recv_sem=recv_sem.at[n], device_id=device, device_id_type=MESH)

    def whole(ref, n):
        return remote(ref, ref, n, (pair ^ 1, tok))

    leaving = []

    def finish():
        for ref, n in leaving:
            whole(ref, n).wait_send()

    sp_copy = pltpu.make_async_copy(sp_hbm, sp, loc_sem.at[2])
    vals_copy = pltpu.make_async_copy(vals_hbm, vals, loc_sem.at[3])
    idx_copy = pltpu.make_async_copy(idx_hbm, idx, loc_sem.at[4])
    tg_copy = pltpu.make_async_copy(tg_hbm, tg_ref, loc_sem.at[5])
    dec_copy = [pltpu.make_async_copy(dec_hbm.at[j], dec.at[j], loc_sem.at[j]) for j in range(2)]
    sp_copy.start()
    vals_copy.start()
    idx_copy.start()
    tg_copy.start()
    dec_copy[0].start()
    dec_copy[1].start()

    barrier = pltpu.get_barrier_semaphore()

    def greet_column(m, _):
        pl.semaphore_signal(barrier, inc=1, device_id=(pair ^ ((m & 4) << 1), tok ^ (m & 3)), device_id_type=MESH)
        return 0

    lax.fori_loop(1, 8, greet_column, 0)

    def greet(k, _):
        pl.semaphore_signal(barrier, inc=1, device_id=(mate(k), tok), device_id_type=MESH)
        return 0

    lax.fori_loop(1, 32, greet, 0)

    sp_copy.wait()
    idx_copy.wait()
    for j in range(2):
        i0[...] = idx[jnp.maximum(sp[0, 2 * pair + j], 0)]
        for gb in range(16):
            rows = i0[pl.ds((gb // 2) * 16 + gb % 2, 8, stride=2), :]
            lo[j, gb * 8:gb * 8 + 8, :] = jnp.bitwise_and(rows, 127)
            hi[j, gb * 8:gb * 8 + 8, :] = lax.shift_right_logical(rows, 7)

    place_maps(0, lo, hi, onehot, inv)

    mine = pl.ds(pl.multiple_of(tok * 32, 32), 32)
    vals_copy.wait()
    for j in range(2):
        v0[j, mine, :] = vals[jnp.maximum(sp[0, 2 * pair + j], 0)]

    pl.semaphore_wait(barrier, 38)

    for d in range(1, 4):
        remote(v0.at[:, mine], v0.at[:, mine], 0, (pair, tok ^ d)).start()
    leaving.append((v0.at[:, pl.ds(0, 96)], 0))


    def group(j, h, i):
        return arrived.at[j, h, pl.ds(i * 8 if i else 1, 8 if i else 7)]

    def send_blocks(j, h, first=1, end=32):
        def send_block(k, _):
            to = mate(k)
            rows = pl.ds(pl.multiple_of((((to >> 4) << 1) | (to & 1)) * RB, RB), RB)
            block = part.at[j, h, (to >> 1) & 3, rows]
            remote(block, arrived.at[j, h, k], 9 + (j * 2 + h) * 4 + (k >> 3), (to, tok)).start()
            return 0

        lax.fori_loop(first, end, send_block, 0, unroll=4)
        if end < 32:
            return
        arrived[j, h, 0] = part[j, h, x, my_rows, :]
        for i in range(4):
            leaving.append((group(j, h, i), 9 + (j * 2 + h) * 4 + i))

    my_rows = pl.ds(pl.multiple_of(((y << 1) | c) * RB, RB), RB)
    for j in range(2):
        if j == 0:
            place_maps(1, lo, hi, onehot, inv)
            whole(v0.at[:, pl.ds(0, 96)], 0).wait_recv()
        vp[...] = v0[j].astype(F32)

        def spread(g, _):
            rows = pl.ds(pl.multiple_of(g * 16, 16), 16)
            values = jnp.concatenate([vp[pl.ds(g * 16 + b, 8, stride=2), :] for b in range(2)], 0)
            for h in range(16):
                place = inv[j, h, rows, :]
                chosen = jnp.take_along_axis(values, jnp.maximum(place - 1, 0), axis=1)
                dense[rows, h * 128:h * 128 + 128] = jnp.where(place > 0, chosen, 0.0).astype(BF16)
            return 0

        lax.fori_loop(0, 8, spread, 0, unroll=4)
        dec_copy[j].wait()
        for px in range(4):
            both = jnp.dot(dense[...], dec[j, :, px * CB:px * CB + CB], preferred_element_type=F32)
            part[j, 0, px] = both[:, :HB]
            part[j, 1, px] = both[:, HB:]
        send_blocks(j, 0)
        if j == 0:
            send_blocks(0, 1, 1, EARLY)
    tg_copy.wait()
    for b in range(8):
        for l in range(L):
            tg[b, 2 * l:2 * l + 2, :] = tg_ref[l, :, b * 128:b * 128 + 128].astype(F32)
        tg[b, 22:24, :] = jnp.zeros((2, 128), F32)

    def send_targets(i, _):
        px = x ^ i
        cols = pl.ds(px * 2, 2)

        @pl.when(i != 0)
        def _():
            remote(tg.at[cols], tgr.at[x * 2 + c], 1, ((pair & 56) | (px << 1) | zh, tok)).start()

        @pl.when(jnp.logical_and(i == 0, c != zh))
        def _():
            remote(tg.at[cols], tgr.at[x * 2 + c], 1, (pair ^ 1, tok)).start()

        @pl.when(jnp.logical_and(i == 0, c == zh))
        def _():
            tgr[x * 2 + c] = tg[cols]

        return 0

    lax.fori_loop(0, 4, send_targets, 0)

    send_blocks(0, 1, EARLY)
    send_blocks(1, 1)

    def turn(j):
        def block(f, _):
            cols = pl.ds(pl.multiple_of(f * 256, 256), 256)
            dect[j, :, cols] = dec[j, cols, :].T
            return 0

        lax.fori_loop(0, 8, block, 0)

    sums[...] = jnp.zeros((2, L, RB, HB), F32)

    @pl.when(c == zh)
    def _():
        whole(tgr.at[pl.ds(0, 7)], 1).wait_recv()
        for l in range(L):
            for b in range(2):
                for h in range(2):
                    sums[h, l, b * 8:b * 8 + 8, :] = -tgr.reshape(8 * 48, 128)[
                        pl.ds(h * 24 + l * 2 + b, 8, stride=48), :]

    turn(0)
    zsem = (7, 2)

    def add_up(h):
        for j in range(2):
            for i in range(4):
                whole(group(j, h, i), 9 + (j * 2 + h) * 4 + i).wait_recv()

                def add(m, totals):
                    target = sp[1, 2 * mate(i * 8 + m) + j]
                    block = arrived[j, h, i * 8 + m]
                    return tuple(t + jnp.where(target == l, block, 0.0) for l, t in enumerate(totals))

                totals = lax.fori_loop(0, 8, add, tuple(sums[h, l] for l in range(L)), unroll=2)
                for l in range(L):
                    sums[h, l] = totals[l]

        def send_layer(l, _):
            remote(sums.at[h, l], sums_z.at[h, l], zsem[h], (pair ^ 8, tok)).start()
            return 0

        lax.fori_loop(0, L, send_layer, 0)
        leaving.append((sums.at[h], zsem[h]))

    def give_back(h):
        whole(sums_z.at[h], zsem[h]).wait_recv()
        for l in range(L):
            resid[h, l] = ((sums[h, l] + sums_z[h, l]) * D ** (-0.5)).astype(BF16)
        my_cols = pl.ds(pl.multiple_of(x * CB + h * HB, HB), HB)
        for j in range(2):
            def give(k, _):
                to = mate(k)
                back[j, k, h] = resid[h, jnp.maximum(sp[1, 2 * to + j], 0)]
                remote(back.at[j, k, h], grad_in.at[j, my_rows, my_cols], 3 + j, (to, tok)).start()
                return 0

            lax.fori_loop(1, 32, give, 0, unroll=4)
            grad_in[j, my_rows, my_cols] = resid[h, jnp.maximum(sp[1, 2 * pair + j], 0)]

    def sent_targets():
        @pl.when(c == zh)
        def _():
            whole(tgr.at[pl.ds(0, 3)], 1).wait_send()

        @pl.when(c != zh)
        def _():
            whole(tgr.at[pl.ds(0, 4)], 1).wait_send()

    add_up(0)
    add_up(1)
    give_back(0)
    turn(1)
    sent_targets()
    give_back(1)
    for j in range(2):
        leaving.append((back.at[j, pl.ds(1, 31)], 3 + j))

    for j in range(2):
        whole(back.at[j, pl.ds(1, 31)], 3 + j).wait_recv()
        picked[...] = jnp.zeros((ROWS, K), F32)

        def features(f, _):
            grads = jnp.dot(grad_in[j], dect[j, :, pl.ds(pl.multiple_of(f * 256, 256), 256)],
                            preferred_element_type=F32)
            for q in range(2):
                chosen = jnp.take_along_axis(grads[:, q * 128:q * 128 + 128], lo[j], axis=1)
                picked[...] = jnp.where(hi[j] == f * 2 + q, chosen, picked[...])
            return 0

        lax.fori_loop(0, 8, features, 0, unroll=4)
        for gb in range(16):
            start = (gb // 4) * 64 + j * 4 + gb % 4
            gsend.reshape(256, K)[pl.ds(start, 8, stride=8), :] = picked[gb * 8:gb * 8 + 8, :]

    def send_picked(k, _):
        to = mate(k)
        q = ((to >> 4) << 3) | (to & 7)
        remote(gsend.at[q], grecv.at[k], 5, (to, tok)).start()
        return 0

    lax.fori_loop(1, 32, send_picked, 0, unroll=4)
    grecv[0] = gsend[(y << 3) | (x << 1) | c]
    leaving.append((grecv.at[pl.ds(1, 31)], 5))
    whole(grecv.at[pl.ds(1, 31)], 5).wait_recv()

    def add_picked(k, totals):
        first = 2 * mate(k)
        upper = lax.broadcasted_iota(I32, (8, K), 0) < 4
        source = jnp.where(upper, sp[0, first], sp[0, first + 1])
        block = grecv[k]
        return tuple(t + jnp.where(source == l, block, 0.0) for l, t in enumerate(totals))

    totals = lax.fori_loop(0, 32, add_picked, tuple(jnp.zeros((8, K), F32) for _ in range(L)), unroll=8)
    for l in range(L):
        both = totals[l][0:4] + totals[l][4:8]
        fin[0, 2 * l:2 * l + 2, :] = both[0:2]
        fin[1, 2 * l:2 * l + 2, :] = both[2:4]
    for z in range(2):
        fin[z, 22:24, :] = jnp.zeros((2, K), F32)

    me = (zh << 2) | tok

    def send_final(m, _):
        remote(fin.at[zh ^ (m >> 2)], fin_r.at[me], 6, (pair ^ ((m & 4) << 1), tok ^ (m & 3))).start()
        return 0

    lax.fori_loop(1, 8, send_final, 0)
    fin_r[me] = fin[zh]
    whole(fin_r.at[pl.ds(0, 7)], 6).wait_recv()
    leaving.append((fin_r.at[pl.ds(0, 7)], 6))
    total = fin_r[0]
    for m in range(1, 8):
        total = total + fin_r[m]
    for l in range(L):
        out[l] = total[2 * l:2 * l + 2]
    finish()


def local(act_vals, act_idx, slot_pairs, decoders, targets):
    hbm, vmem = pl.BlockSpec(memory_space=pltpu.HBM), pl.BlockSpec(memory_space=pltpu.VMEM)
    return pl.pallas_call(
        kernel,
        out_shape=jax.ShapeDtypeStruct((L, 2, K), F32),
        in_specs=[hbm] * 5,
        out_specs=vmem,
        scratch_shapes=[
            pltpu.SMEM((2, 128), I32),
            pltpu.VMEM((L, 32, K), BF16),
            pltpu.VMEM((L, ROWS, K), I32),
            pltpu.VMEM((L, 2, DC), BF16),
            pltpu.VMEM((2, F, DC), BF16),
            pltpu.VMEM((2, ROWS, K), BF16),
            pltpu.VMEM((ROWS, K), I32),
            pltpu.VMEM((ROWS, K), F32),
            pltpu.VMEM((2, ROWS, K), I32),
            pltpu.VMEM((2, ROWS, K), I32),
            pltpu.VMEM((ROWS * 16, K), F32),
            pltpu.VMEM((2, 16, ROWS, K), I32),
            pltpu.VMEM((ROWS, F), BF16),
            pltpu.VMEM((2, DC, F), BF16),
            pltpu.VMEM((2, 2, 4, ROWS, HB), F32),
            pltpu.VMEM((2, 2, 32, RB, HB), F32),
            pltpu.VMEM((8, 24, 128), F32),
            pltpu.VMEM((8, 2, 24, 128), F32),
            pltpu.VMEM((2, L, RB, HB), F32),
            pltpu.VMEM((2, L, RB, HB), F32),
            pltpu.VMEM((2, L, RB, HB), BF16),
            pltpu.VMEM((2, 32, 2, RB, HB), BF16),
            pltpu.VMEM((2, ROWS, DC), BF16),
            pltpu.VMEM((ROWS, K), F32),
            pltpu.VMEM((32, 8, K), F32),
            pltpu.VMEM((32, 8, K), F32),
            pltpu.VMEM((2, 24, K), F32),
            pltpu.VMEM((8, 24, K), F32),
            pltpu.SemaphoreType.DMA((6,)),
            pltpu.SemaphoreType.DMA((25,)),
            pltpu.SemaphoreType.DMA((25,)),
        ],
        compiler_params=pltpu.CompilerParams(collective_id=0, has_side_effects=True, vmem_limit_bytes=60 << 20),
        cost_estimate=pl.CostEstimate(flops=2 * 2 * 2 * ROWS * F * DC, bytes_accessed=10 << 20, transcendentals=0),
        name="transcoder",
    )(slot_pairs.T, act_vals, act_idx, decoders, targets)


def solution(mesh):
    return jax.shard_map(
        local,
        mesh=mesh,
        in_specs=(P(None, "tok", None), P(), P(), P("pair", None, "tok"), P(None, "pair", "tok")),
        out_specs=P(None, "pair", None),
        check_vma=False,
    )
```
